512 devices in a mesh: rows: 128 (over y, z_hi, x), cols: 4 (over z_lo, core).
Axes of the slice: x: 4, y: 8, z: 8 (z_hi: 4, z_lo: 2; z = z_hi * 2 + z_lo), core: 2. Of those that a mesh axis runs over, the one named last changes fastest.
Arguments:
- fine_noisy: bfloat16 [1024, 128, 256], P('rows', 'cols'), may hold values from -6 to 6
- fine_weight: bfloat16 [2304, 256], P(None, 'cols'), may hold values from -0.125 to 0.125
- projection: bfloat16 [512, 256], P(None, 'cols'), may hold values from -0.25 to 0.25
- mid_noisy: bfloat16 [256, 32, 512], P('rows', 'cols'), may hold values from -6 to 6
- teacher_weight: bfloat16 [4608, 512], P(None, 'cols'), may hold values from -0.09375 to 0.09375
- student_weight: bfloat16 [4608, 512], P(None, 'cols'), may hold values from -0.09375 to 0.09375
- steps: int32 [3], replicated, may hold values from 401 to 999, as said below
- cotangent: bfloat16 [1024, 128, 256], P('rows', 'cols'), may hold values from -6 to 6
Outputs:
- fine_out: bfloat16 [1024, 128, 256], P('rows', 'cols')
- grad_input: bfloat16 [1024, 128, 256], P('rows', 'cols')
- grad_weight: float32 [2304, 256], P('rows')
- gap: bfloat16 [256, 32, 512], P('rows', 'cols')
The draws below stay inside these ranges and needn't reach their ends.
Inputs may be any that keep to these rules, and one draw needn't show every extreme that they name: steps[0] is 999; each later index lies 150 to 299 below the one before it.
All inputs are finite; a program needn't handle non-finite values.
Results may differ from the reference program's by a relative error of at most 0.012.
Values may be sent and summed in bfloat16 or wider, within the bound.
No kernel may reach another device: no remote copies, remote signals or barrier semaphores. Data moves between devices by JAX's collectives and lax.ppermute only.
A program may use at most 64 MiB of HBM per device.

```python
import math
import jax
import jax.numpy as jnp
from jax import lax

C = 256
CM = 512
H = 1024
W = 128
HM = 256
WM = 32


def draw_steps(key, part):
    key = jax.random.fold_in(key, 5)
    keys = jax.random.split(key, 2)
    second = 999 - jax.random.randint(keys[0], (), 150, 300)
    third = second - jax.random.randint(keys[1], (), 150, 300)
    return jnp.stack([jnp.array(999, jnp.int32), second, third]).astype(jnp.int32)


def block_levels(stream_key, dims, pieces, least, largest):
    def one(axis_at, shards_of):
        draws = jax.random.uniform(jax.random.fold_in(jax.random.fold_in(stream_key, 6), axis_at), (shards_of,), jnp.float32, least / len(pieces), largest / len(pieces))
        return jnp.repeat(jnp.exp(draws), dims[axis_at] // shards_of).reshape((-1,) + (1,) * (len(dims) - axis_at - 1))

    gain = one(*pieces[0])
    for cut in pieces[1:]:
        gain = gain * one(*cut)
    return gain


def bell_draw(stream_key, extent, deviation, most, shards=(), kind=jnp.bfloat16):
    gain = block_levels(stream_key, extent, shards, -0.22, 0.18) if shards else 1.0
    drawn = jax.random.normal(stream_key, extent, jnp.float32) * deviation * gain
    return jnp.minimum(jnp.maximum(drawn, -most), most).astype(kind)


def setup_inputs(seed: int = 0) -> dict:
    arg_keys = jax.random.split(jax.random.key(seed), 9)
    fine_noisy = bell_draw(arg_keys[0], (H, W, C), 1.0, 6.0, ((0, 128), (1, 4)))
    fine_weight = bell_draw(arg_keys[1], (9 * C, C), (9 * C) ** -0.5, 0.125, ((1, 4),))
    projection = bell_draw(arg_keys[2], (CM, C), CM ** -0.5, 0.25, ((1, 4),))
    mid_noisy = bell_draw(arg_keys[3], (HM, WM, CM), 1.0, 6.0, ((0, 128), (1, 4)))
    teacher_weight = bell_draw(arg_keys[4], (9 * CM, CM), (9 * CM) ** -0.5, 0.09375, ((1, 4),))
    student_weight = bell_draw(arg_keys[5], (9 * CM, CM), (9 * CM) ** -0.5, 0.09375, ((1, 4),))
    steps = draw_steps(jax.random.fold_in(arg_keys[8], 71), 0)
    cotangent = bell_draw(arg_keys[7], (H, W, C), 1.0, 6.0, ((0, 128), (1, 4)))
    return {"fine_noisy": fine_noisy, "fine_weight": fine_weight, "projection": projection, "mid_noisy": mid_noisy, "teacher_weight": teacher_weight, "student_weight": student_weight, "steps": steps, "cotangent": cotangent}


def embed(step_index, channels):
    half = channels // 2
    freqs = jnp.exp(-math.log(10000.0) * jnp.arange(half).astype(jnp.float32) / half)
    angles = step_index.astype(jnp.float32) * freqs
    return jnp.concatenate([jnp.sin(angles), jnp.cos(angles)])

def conv(field, weight):
    channels = field.shape[-1]
    kernel = weight.reshape(3, 3, channels, weight.shape[-1])
    result = lax.conv_general_dilated(field[None], kernel, (1, 1), ((1, 1), (1, 1)), dimension_numbers=('NHWC', 'HWIO', 'NHWC'), preferred_element_type=jnp.float32)
    return result[0]

def flipped(weight):
    channels = weight.shape[-1]
    blocks = weight.reshape(9, channels, channels)[::-1]
    return jnp.transpose(blocks, (0, 2, 1)).reshape(9 * channels, channels)

def reference(fine_noisy, fine_weight, projection, mid_noisy, teacher_weight, student_weight, steps, cotangent):
    channels = mid_noisy.shape[-1]
    times = steps.astype(jnp.float32)
    delta_one = (times[1] - times[0]) / 1000.0
    delta_two = (times[2] - times[1]) / 1000.0
    anchor = mid_noisy.astype(jnp.float32)
    first_in = jax.nn.silu(anchor + embed(steps[0], channels)).astype(jnp.bfloat16)
    teacher_one = conv(first_in, teacher_weight)
    student_one = conv(first_in, student_weight)
    middle = anchor + delta_one * teacher_one
    second_in = jax.nn.silu(middle + embed(steps[1], channels)).astype(jnp.bfloat16)
    teacher_two = conv(second_in, teacher_weight)
    target = middle + delta_two * teacher_two
    gap = (target - (anchor + (delta_one + delta_two) * student_one)).astype(jnp.bfloat16)
    fine_ch = fine_noisy.shape[-1]
    lifted = jnp.dot(target.astype(jnp.bfloat16).reshape(-1, channels), projection, preferred_element_type=jnp.float32)
    lifted = lifted.reshape(target.shape[0], target.shape[1], fine_ch)
    lifted = jnp.repeat(jnp.repeat(lifted, 4, axis=0), 4, axis=1)
    fine_in = (fine_noisy.astype(jnp.float32) + lifted).astype(jnp.bfloat16)
    fine_out = conv(fine_in, fine_weight).astype(jnp.bfloat16)
    grad_input = conv(cotangent, flipped(fine_weight)).astype(jnp.bfloat16)
    height, width = (fine_in.shape[0], fine_in.shape[1])
    padded = jnp.pad(fine_in, ((1, 1), (1, 1), (0, 0)))
    cot_flat = cotangent.reshape(-1, fine_ch)
    blocks = []
    for row_shift in range(3):
        for col_shift in range(3):
            shifted = padded[row_shift:row_shift + height, col_shift:col_shift + width].reshape(-1, fine_ch)
            blocks.append(jnp.dot(shifted.T, cot_flat, preferred_element_type=jnp.float32))
    grad_weight = jnp.concatenate(blocks, axis=0) / math.sqrt(height * width)
    return (fine_out, grad_input, grad_weight, gap)
```

```python
import math

import jax
import jax.numpy as jnp
import numpy as np
from jax import lax
from jax.experimental import pallas as pl
from jax.experimental.pallas import tpu as pltpu
from jax.sharding import PartitionSpec as P

BF = jnp.bfloat16
F32 = jnp.float32
MIB = 1024 * 1024


def call(body, outs, scratch, flops, vmem, name, n_in):
    return pl.pallas_call(
        body,
        out_shape=outs,
        in_specs=[pl.BlockSpec(memory_space=pltpu.VMEM)] * n_in,
        out_specs=[pl.BlockSpec(memory_space=pltpu.VMEM)] * len(outs),
        scratch_shapes=scratch,
        compiler_params=pltpu.CompilerParams(vmem_limit_bytes=vmem * MIB),
        cost_estimate=pl.CostEstimate(flops=flops, bytes_accessed=4 * MIB, transcendentals=0),
        name=name,
    )


def shape(dims, kind):
    return jax.ShapeDtypeStruct(dims, kind)


def silu(value):
    return value * (1.0 / (1.0 + jnp.exp(-value)))


def shifted(field, step):
    if step == 0:
        return field
    edge = jnp.zeros((field.shape[0], 1, field.shape[2]), field.dtype)
    if step < 0:
        return jnp.concatenate([edge, field[:, :-1]], axis=1)
    return jnp.concatenate([field[:, 1:], edge], axis=1)


def pack_kernel(fine_ref, cot_ref, weight_ref, proj_ref, mid_ref, bulk_ref, down_ref, up_ref, own_ref):
    bulk_ref[0:256, :] = fine_ref[...]
    bulk_ref[256:512, :] = cot_ref[...]
    for tap in range(9):
        base = tap * 256
        bulk_ref[512 + 64 * tap : 576 + 64 * tap, :] = jnp.concatenate(
            [weight_ref[base + 64 * q : base + 64 * q + 64, :] for q in range(4)], axis=1
        )
    bulk_ref[1088:1216, :] = jnp.concatenate(
        [proj_ref[128 * q : 128 * q + 128, :] for q in range(4)], axis=1
    )
    low, high = mid_ref[:, 0:256], mid_ref[:, 256:512]
    for ref in (down_ref, up_ref, own_ref):
        ref[0:16, :] = low
        ref[16:32, :] = high
    down_ref[32:64, :] = cot_ref[224:256, :]
    up_ref[32:64, :] = cot_ref[0:32, :]


def first_kernel(near_ref, teacher_ref, student_ref, coef_ref, sec_ref, mid_ref, base_ref, raw_ref, in_ref):
    row, col = lax.axis_index("rows"), lax.axis_index("cols")
    last = lax.axis_size("rows") - 1
    tiles = [near_ref[s].astype(F32) for s in range(4)]
    lines = []
    for start, half in ((0, 0), (0, 8), (128, 0), (128, 8), (64, 0), (64, 8)):
        at = start + half
        lines.append(
            jnp.concatenate(
                [jnp.concatenate([t[at : at + 8], t[at + 16 : at + 24]], axis=1) for t in tiles], axis=0
            )
        )
    raw = jnp.stack(lines)
    raw_ref[...] = raw.reshape(192, 512)
    lit = silu(raw + coef_ref[0:1, :].reshape(1, 1, 512))
    line = lax.broadcasted_iota(jnp.int32, (6, 32, 512), 0)
    inside = ((line >= 2) | (row > 0)) & ((line < 4) | (row < last))
    lit = jnp.where(inside, lit, 0.0)
    for at, step in enumerate((-1, 0, 1)):
        in_ref[at] = shifted(lit, step).astype(BF).reshape(192, 512)
    total = jnp.zeros((128, 256), F32)
    for dy in range(3):
        for dx in range(3):
            k = (3 * dy + dx) * 512
            both = jnp.concatenate([teacher_ref[k : k + 512, :], student_ref[k : k + 512, :]], axis=1)
            total += jnp.dot(in_ref[dx, 32 * dy : 32 * dy + 128, :], both, preferred_element_type=F32)
    own = pl.ds(pl.multiple_of(col * 128, 128), 128)
    anchor = raw_ref[32:160, own]
    one, two = coef_ref[2:3, 0:128], coef_ref[3:4, 0:128]
    middle = anchor + one * total[:, 0:128]
    second = silu(middle + coef_ref[1:2, own])
    line = lax.broadcasted_iota(jnp.int32, (128, 128), 0)
    inside = ((line >= 32) | (row > 0)) & ((line < 96) | (row < last))
    sec_ref[...] = jnp.where(inside, second, 0.0).astype(BF)
    mid_ref[...] = middle[32:96]
    base_ref[...] = anchor[32:96] + (one + two) * total[32:96, 128:256]


def second_kernel(sec_ref, teacher_ref, mid_ref, base_ref, coef_ref, out_ref, in_ref):
    field = jnp.concatenate([sec_ref[s] for s in range(4)], axis=1).astype(F32).reshape(4, 32, 512)
    for at, step in enumerate((-1, 0, 1)):
        in_ref[at] = shifted(field, step).astype(BF).reshape(128, 512)
    total = jnp.zeros((64, 128), F32)
    for dy in range(3):
        for dx in range(3):
            k = (3 * dy + dx) * 512
            total += jnp.dot(
                in_ref[dx, 32 * dy : 32 * dy + 64, :], teacher_ref[k : k + 512, :], preferred_element_type=F32
            )
    target = mid_ref[...] + coef_ref[3:4, 0:128] * total
    out_ref[0:64, :] = target.astype(BF)
    out_ref[64:128, :] = (target - base_ref[...]).astype(BF)


def grad_kernel(bulk_ref, near_ref, late_ref, part_ref, field_ref, gap_ref, sum_ref, gap_scratch):
    col = lax.axis_index("cols")
    target = jnp.concatenate([late_ref[s, 0:64, :] for s in range(4)], axis=1)
    place = lax.broadcasted_iota(jnp.int32, (128, 32), 0) // 4
    repeat = (place == lax.broadcasted_iota(jnp.int32, (128, 32), 1)).astype(BF)
    proj = jnp.concatenate(
        [
            jnp.concatenate([bulk_ref[s, 1088:1216, 64 * q : 64 * q + 64] for s in range(4)], axis=1)
            for q in range(4)
        ],
        axis=0,
    )
    for m in range(2):
        wide = jnp.dot(repeat, target[32 * m : 32 * m + 32], preferred_element_type=F32).astype(BF)
        lifted = jnp.dot(wide, proj, preferred_element_type=F32)
        for i in range(4 * m, 4 * m + 4):
            noisy = jnp.concatenate([bulk_ref[s, 32 * i : 32 * i + 32, :] for s in range(4)], axis=0)
            field_ref[128 * i : 128 * i + 128, :] = (noisy.astype(F32) + lifted).astype(BF)
    pair = pl.ds(pl.multiple_of((col // 2) * 128, 128), 128)
    lines = [near_ref[s, 32:64, pair] for s in range(4)]
    for i in range(8):
        lines += [bulk_ref[s, 256 + 32 * i : 288 + 32 * i, pair] for s in range(4)]
    lines += [near_ref[s, 96:128, pair] for s in range(4)]
    cot = jnp.concatenate(lines, axis=0).astype(F32)
    cot = jnp.where(col % 2 == 1, cot[:, 64:128], cot[:, 0:64]).reshape(10, 128, 64)
    moved = jnp.concatenate([shifted(cot, -dx) for dx in (-1, 0, 1)], axis=2).astype(BF).reshape(1280, 192)
    field = field_ref[...]
    for dy in (-1, 0, 1):
        term = lax.dot_general(
            field,
            moved[(1 - dy) * 128 : (1 - dy) * 128 + 1024],
            (((0,), (0,)), ((), ())),
            preferred_element_type=F32,
        )
        for dx in range(3):
            one = term[:, 64 * dx : 64 * dx + 64]
            at = (3 * (dy + 1) + dx) * 256
            sum_ref[at : at + 256, :] = jnp.concatenate([one, one], axis=1)
    owners, width = part_ref.shape
    each = 2304 // owners
    lane = lax.broadcasted_iota(jnp.int32, (owners, 128), 1)
    for j in range(width // 128):
        even = sum_ref[pl.ds(2 * j, owners, stride=each), :]
        odd = sum_ref[pl.ds(2 * j + 1, owners, stride=each), :]
        part_ref[:, 128 * j : 128 * j + 128] = jnp.where(lane < 64, even, odd).astype(BF)
    gap_scratch[...] = jnp.concatenate([late_ref[s, 64:128, :] for s in range(4)], axis=1).astype(F32)
    gap_ref[...] = jnp.concatenate(
        [gap_scratch[pl.ds(pl.multiple_of(32 * i + 8 * col, 8), 8), :] for i in range(2)], axis=0
    ).astype(BF)


def fine_kernel(bulk_ref, near_ref, field_ref, above_ref, below_ref, out_ref, back_ref, weight_ref, in_ref):
    col = lax.axis_index("cols")
    for tap in range(9):
        at = 512 + 64 * tap
        for q in range(4):
            weight_ref[256 * tap + 64 * q : 256 * tap + 64 * q + 64, :] = jnp.concatenate(
                [bulk_ref[s, at : at + 64, 64 * q : 64 * q + 64] for s in range(4)], axis=1
            )
    start = pl.multiple_of(32 * col, 32)
    before = pl.multiple_of(jnp.maximum(32 * col - 16, 0), 16)
    after = pl.multiple_of(jnp.minimum(32 * col + 32, 112), 16)

    def window(ref, base):
        left = ref[pl.ds(base + before, 16), :].astype(F32)
        right = ref[pl.ds(base + after, 16), :].astype(F32)
        return jnp.concatenate(
            [
                jnp.where(col > 0, left, 0.0),
                ref[pl.ds(base + start, 32), :].astype(F32),
                jnp.where(col < 3, right, 0.0),
            ],
            axis=0,
        )

    wide = jnp.stack(
        [window(above_ref, 0)] + [window(field_ref, 128 * i) for i in range(8)] + [window(below_ref, 0)]
    )
    for at in range(3):
        in_ref[at] = wide[:, 15 + at : 47 + at].astype(BF).reshape(320, 256)
    total = jnp.zeros((256, 256), F32)
    for dy in range(3):
        for dx in range(3):
            k = (3 * dy + dx) * 256
            total += jnp.dot(
                in_ref[dx, 32 * dy : 32 * dy + 256, :], weight_ref[k : k + 256, :], preferred_element_type=F32
            )
    out_ref[...] = total.astype(BF)

    left_tile, right_tile = jnp.maximum(col - 1, 0), jnp.minimum(col + 1, 3)

    def cot_window(ref, at):
        left = ref[left_tile, at + 16 : at + 32, :].astype(F32)
        right = ref[right_tile, at : at + 16, :].astype(F32)
        return jnp.concatenate(
            [
                jnp.where(col > 0, left, 0.0),
                ref[col, at : at + 32, :].astype(F32),
                jnp.where(col < 3, right, 0.0),
            ],
            axis=0,
        )

    wide = jnp.stack(
        [cot_window(near_ref, 32)]
        + [cot_window(bulk_ref, 256 + 32 * i) for i in range(8)]
        + [cot_window(near_ref, 96)]
    )
    for at in range(3):
        in_ref[at] = wide[:, 15 + at : 47 + at].astype(BF).reshape(320, 256)
    total = jnp.zeros((256, 256), F32)
    for dy in range(3):
        for dx in range(3):
            k = (3 * dy + dx) * 256
            total += lax.dot_general(
                in_ref[2 - dx, 32 * (2 - dy) : 32 * (2 - dy) + 256, :],
                weight_ref[k : k + 256, :],
                (((1,), (1,)), ((), ())),
                preferred_element_type=F32,
            )
    back_ref[...] = total.astype(BF)


def on_device(
    fine_noisy, fine_weight, projection, mid_noisy, teacher_weight, student_weight, steps, cotangent
):
    count = lax.axis_size("rows")
    forward = [(i, i + 1) for i in range(count - 1)]
    backward = [(i + 1, i) for i in range(count - 1)]

    bulk, down, up, own = call(
        pack_kernel,
        [shape((1216, 256), BF), shape((64, 256), BF), shape((64, 256), BF), shape((32, 256), BF)],
        [],
        MIB,
        16,
        "pack",
        5,
    )(
        fine_noisy.reshape(256, 256),
        cotangent.reshape(256, 256),
        fine_weight,
        projection,
        mid_noisy.reshape(16, 512),
    )
    bulk = lax.all_gather(bulk, "cols", axis=0)
    above = lax.ppermute(down, "rows", forward)
    below = lax.ppermute(up, "rows", backward)

    freqs = jnp.asarray(np.exp(-math.log(10000.0) * np.arange(256, dtype=np.float32) / 256).astype(np.float32))
    times = steps.astype(F32)
    angles = times[0:2, None] * freqs[None, :]
    waves = jnp.concatenate([jnp.sin(angles), jnp.cos(angles)], axis=1)
    deltas = jnp.broadcast_to(((times[1:3] - times[0:2]) / 1000.0)[:, None], (2, 512))
    coef = jnp.concatenate([waves, deltas], axis=0)

    near = lax.all_gather(jnp.concatenate([above, below, own], axis=0), "cols", axis=0)
    sec, middle, base = call(
        first_kernel,
        [shape((128, 128), BF), shape((64, 128), F32), shape((64, 128), F32)],
        [pltpu.VMEM((192, 512), F32), pltpu.VMEM((3, 192, 512), BF)],
        300 * MIB,
        16,
        "first",
        4,
    )(near, teacher_weight, student_weight, coef)
    sec = lax.all_gather(sec, "cols", axis=0)
    (late,) = call(
        second_kernel,
        [shape((128, 128), BF)],
        [pltpu.VMEM((3, 128, 512), BF)],
        100 * MIB,
        16,
        "second",
        5,
    )(sec, teacher_weight, middle, base, coef)
    late = lax.all_gather(late, "cols", axis=0)
    part, field, gap = call(
        grad_kernel,
        [shape((count, 64 * 2304 // count), BF), shape((1024, 256), BF), shape((16, 512), BF)],
        [pltpu.VMEM((2304, 128), F32), pltpu.VMEM((64, 512), F32)],
        1000 * MIB,
        32,
        "grad",
        3,
    )(bulk, near, late)
    over = lax.ppermute(field[896:1024], "rows", forward)
    under = lax.ppermute(field[0:128], "rows", backward)
    part = lax.all_to_all(part, "rows", 0, 0, tiled=True)
    share = jnp.sum(part.astype(F32), axis=0) * (1.0 / math.sqrt(1024 * count))
    share = share.reshape(2304 // count, 64)
    grad_weight = lax.all_gather(share, "cols", axis=1, tiled=True)
    fine_out, grad_input = call(
        fine_kernel,
        [shape((256, 256), BF), shape((256, 256), BF)],
        [pltpu.VMEM((2304, 256), BF), pltpu.VMEM((3, 320, 256), BF)],
        1000 * MIB,
        32,
        "fine",
        5,
    )(bulk, near, field, over, under)
    return (
        fine_out.reshape(8, 32, 256),
        grad_input.reshape(8, 32, 256),
        grad_weight,
        gap.reshape(2, 8, 512),
    )


def solution(mesh):
    placed = (
        P("rows", "cols", None),
        P(None, "cols"),
        P(None, "cols"),
        P("rows", "cols", None),
        P(None, "cols"),
        P(None, "cols"),
        P(),
        P("rows", "cols", None),
    )
    return jax.shard_map(
        on_device,
        mesh=mesh,
        in_specs=placed,
        out_specs=(
            P("rows", "cols", None),
            P("rows", "cols", None),
            P("rows", None),
            P("rows", "cols", None),
        ),
        check_vma=False,
    )
```

```python
import functools
import math

import jax
import jax.numpy as jnp
from jax import lax
from jax.experimental import pallas as pl
from jax.experimental.pallas import tpu as pltpu
from jax.sharding import PartitionSpec as P

BF = jnp.bfloat16
F32 = jnp.float32
MIB = 1024 * 1024


def call(body, outs, scratch, flops, vmem, name, ins, out_spaces=None):
    out_spaces = out_spaces or [pltpu.VMEM] * len(outs)
    return pl.pallas_call(
        body,
        out_shape=outs,
        in_specs=[pl.BlockSpec(memory_space=space) for space in ins],
        out_specs=[pl.BlockSpec(memory_space=space) for space in out_spaces],
        scratch_shapes=scratch,
        compiler_params=pltpu.CompilerParams(vmem_limit_bytes=vmem * MIB),
        cost_estimate=pl.CostEstimate(flops=flops, bytes_accessed=MIB, transcendentals=0),
        name=name,
    )


def shape(dims, kind):
    return jax.ShapeDtypeStruct(dims, kind)


def silu(value):
    return value * (1.0 / (1.0 + jnp.exp(-value)))


def shifted(field, step):
    if step == 0:
        return field
    edge = jnp.zeros((field.shape[0], 1, field.shape[2]), field.dtype)
    if step < 0:
        return jnp.concatenate([edge, field[:, :-1]], axis=1)
    return jnp.concatenate([field[:, 1:], edge], axis=1)


def pack_kernel(cot_ref, mid_ref, one_ref, two_ref, sems):
    even = lax.axis_index("rows") % 2 == 0
    last, first = pl.multiple_of(jnp.where(even, 224, 0), 32), pl.multiple_of(jnp.where(even, 0, 224), 32)
    moves = [
        (mid_ref.at[:, 256 * half : 256 * half + 256], ref.at[16 * half : 16 * half + 16, :])
        for ref in (one_ref, two_ref)
        for half in range(2)
    ]
    moves += [
        (cot_ref.at[pl.ds(last, 32), :], one_ref.at[32:64, :]),
        (cot_ref.at[pl.ds(first, 32), :], two_ref.at[32:64, :]),
    ]
    for copy in start_all(moves, sems):
        copy.wait()


def near_at(row):
    even = row % 2 == 0
    above = pl.multiple_of(jnp.where(even, 128, 0), 64)
    below = pl.multiple_of(jnp.where(even, 64, 128), 64)
    return above, below, pl.multiple_of(jnp.where(even, 0, 64), 64)


def start_all(moves, sems):
    copies = [pltpu.make_async_copy(src, dst, sems.at[n]) for n, (src, dst) in enumerate(moves)]
    for copy in copies:
        copy.start()
    return copies


def waves(angle):
    turns = jnp.round(angle * (0.5 / math.pi))
    rest = (angle - turns * 6.28125) - turns * (2 * math.pi - 6.28125)
    square = rest * rest
    sin, cos = jnp.ones_like(rest), jnp.ones_like(rest)
    for n in range(9, 0, -1):
        cos = 1.0 - square * cos * (1.0 / ((2 * n - 1) * (2 * n)))
        sin = 1.0 - square * sin * (1.0 / ((2 * n) * (2 * n + 1)))
    return rest * sin, cos


def embed(step):
    index = lax.broadcasted_iota(jnp.int32, (1, 256), 1)
    freqs = jnp.ones((1, 256), F32)
    for bit in range(8):
        factor = math.exp(-math.log(10000.0) * 2**bit / 256)
        freqs = jnp.where((index // 2**bit) % 2 == 1, freqs * factor, freqs)
    return jnp.concatenate(waves(step.astype(F32) * freqs), axis=1)


def delta(steps_ref, n):
    return (steps_ref[:, n + 1 : n + 2] - steps_ref[:, n : n + 1]).astype(F32) / 1000.0


def first_kernel(
    near_ref, teacher_ref, pupil_ref, steps_ref, cot_ref, proj_ref,
    sec_ref, mid_ref, base_ref,
    tile_ref, raw_ref, wave_ref, in_ref, sems,
):
    row, col = lax.axis_index("rows"), lax.axis_index("cols")
    last = lax.axis_size("rows") - 1
    above, below, own = near_at(row)
    moves = [(near_ref.at[:, pl.ds(start, 32), :], tile_ref.at[n]) for n, start in enumerate((above, own, below))]
    moves += [
        (cot_ref.at[:, 128 * n : 128 * n + 128], sec_ref.at[128 + 256 * n : 384 + 256 * n, :]) for n in range(2)
    ]
    moves += [
        (proj_ref.at[:, 128 * n : 128 * n + 128], sec_ref.at[640 + 64 * n : 704 + 64 * n, :]) for n in range(4)
    ]
    copies = start_all(moves, sems)
    for n in range(2):
        wave_ref[n : n + 1, :] = embed(steps_ref[:, n : n + 1])
    lines = []
    for n in range(3):
        copies[n].wait()
        tiles = [tile_ref[n, s].astype(F32) for s in range(4)]
        for half in (0, 8):
            lines.append(
                jnp.concatenate(
                    [jnp.concatenate([t[half : half + 8], t[half + 16 : half + 24]], axis=1) for t in tiles],
                    axis=0,
                )
            )
    raw = jnp.stack(lines)
    raw_ref[...] = raw.reshape(192, 512)
    lit = silu(raw + wave_ref[0:1, :].reshape(1, 1, 512))
    line = lax.broadcasted_iota(jnp.int32, (6, 32, 512), 0)
    inside = ((line >= 2) | (row > 0)) & ((line < 4) | (row < last))
    lit = jnp.where(inside, lit, 0.0)
    for at, step in enumerate((-1, 0, 1)):
        in_ref[at] = shifted(lit, step).astype(BF).reshape(192, 512)
    total = jnp.zeros((128, 128), F32)
    for dy in range(3):
        for dx in range(3):
            k = (3 * dy + dx) * 512
            total += jnp.dot(
                in_ref[dx, 32 * dy : 32 * dy + 128, :], teacher_ref[k : k + 512, :], preferred_element_type=F32
            )
    own = pl.ds(pl.multiple_of(col * 128, 128), 128)
    anchor = raw_ref[32:160, own]
    one, two = delta(steps_ref, 0), delta(steps_ref, 1)
    middle = anchor + one * total
    second = silu(middle + wave_ref[1:2, own])
    line = lax.broadcasted_iota(jnp.int32, (128, 128), 0)
    inside = ((line >= 32) | (row > 0)) & ((line < 96) | (row < last))
    sec_ref[0:128, :] = jnp.where(inside, second, 0.0).astype(BF)
    mid_ref[...] = middle[32:96]
    total = jnp.zeros((64, 128), F32)
    for dy in range(3):
        for dx in range(3):
            k = (3 * dy + dx) * 512
            total += jnp.dot(
                in_ref[dx, 32 * dy + 32 : 32 * dy + 96, :], pupil_ref[k : k + 512, :], preferred_element_type=F32
            )
    base_ref[...] = anchor[32:96] + (one + two) * total
    for copy in copies[3:]:
        copy.wait()


def weight_moves(turned_ref, first, out_ref, base):
    return [
        (turned_ref.at[:, 128 * (first + n) : 128 * (first + n) + 128], out_ref.at[base + 64 * n : base + 64 * n + 64, :])
        for n in range(9)
    ]


def second_kernel(sec_ref, teacher_ref, mid_ref, base_ref, steps_ref, turned_ref, out_ref, in_ref, sems):
    copies = start_all(weight_moves(turned_ref, 0, out_ref, 128), sems)
    field = jnp.concatenate([sec_ref[s, 0:128, :] for s in range(4)], axis=1).astype(F32).reshape(4, 32, 512)
    for at, step in enumerate((-1, 0, 1)):
        in_ref[at] = shifted(field, step).astype(BF).reshape(128, 512)
    total = jnp.zeros((64, 128), F32)
    for dy in range(3):
        for dx in range(3):
            k = (3 * dy + dx) * 512
            total += jnp.dot(
                in_ref[dx, 32 * dy : 32 * dy + 64, :], teacher_ref[k : k + 512, :], preferred_element_type=F32
            )
    target = mid_ref[...] + delta(steps_ref, 1) * total
    out_ref[0:64, :] = target.astype(BF)
    out_ref[64:128, :] = (target - base_ref[...]).astype(BF)
    for copy in copies:
        copy.wait()


def repeater():
    place = lax.broadcasted_iota(jnp.int32, (128, 32), 0) // 4
    return (place == lax.broadcasted_iota(jnp.int32, (128, 32), 1)).astype(BF)


def lifted(target, proj):
    wide = jnp.dot(repeater(), target, preferred_element_type=F32).astype(BF)
    return lax.dot_general(wide, proj, (((1,), (1,)), ((), ())), preferred_element_type=F32)


def grad_kernel(
    near_ref, sec_ref, late_ref, part_ref, field_ref, one_ref, two_ref, gap_ref, line_ref, sum_ref, gap_scratch
):
    row, col = lax.axis_index("rows"), lax.axis_index("cols")
    above, below, _ = near_at(row)
    even = row % 2 == 0
    pair = pl.multiple_of((col // 2) * 128, 128)
    lanes = pl.ds(pair, 128)
    target = jnp.concatenate([late_ref[s, 0:64, :] for s in range(4)], axis=1)
    proj = jnp.concatenate(
        [
            jnp.concatenate([sec_ref[s, 640 + 64 * n : 704 + 64 * n, :] for n in range(4)], axis=1)
            for s in range(4)
        ],
        axis=0,
    )
    for m in range(2):
        lift = lifted(target[32 * m : 32 * m + 32], proj)
        for i in range(4 * m, 4 * m + 4):
            noisy = jnp.concatenate([near_ref[s, 192 + 32 * i : 224 + 32 * i, :] for s in range(4)], axis=0)
            line_ref[128 * i : 128 * i + 128, :] = (noisy.astype(F32) + lift).astype(BF)
    begin = pl.multiple_of(32 * col, 32)
    before = pl.multiple_of(jnp.maximum(32 * col - 16, 0), 16)
    after = pl.multiple_of(jnp.minimum(32 * col + 32, 112), 16)
    for i in range(8):
        for at, to, size in ((before, 0, 16), (begin, 16, 32), (after, 48, 16)):
            field_ref[i, to : to + size, :] = line_ref[pl.ds(128 * i + at, size), :]
    one_ref[...] = jnp.where(even, line_ref[896:1024, :], line_ref[0:128, :])
    two_ref[...] = jnp.where(even, line_ref[0:128, :], line_ref[896:1024, :])
    gap_scratch[...] = jnp.concatenate([late_ref[s, 64:128, :] for s in range(4)], axis=1).astype(F32)
    gap_ref[...] = jnp.concatenate(
        [gap_scratch[pl.ds(pl.multiple_of(32 * i + 8 * col, 8), 8), :] for i in range(2)], axis=0
    ).astype(BF)
    lines = [near_ref[s, pl.ds(above + 32, 32), lanes] for s in range(4)]
    for i in range(8):
        lines += [sec_ref[s, pl.ds(128 + 32 * i + 2 * pair, 32), :] for s in range(4)]
    lines += [near_ref[s, pl.ds(below + 32, 32), lanes] for s in range(4)]
    cot = jnp.concatenate(lines, axis=0).astype(F32)
    cot = jnp.where(col % 2 == 1, cot[:, 64:128], cot[:, 0:64]).reshape(10, 128, 64)
    moved = jnp.concatenate([shifted(cot, -dx) for dx in (-1, 0, 1)], axis=2).astype(BF).reshape(1280, 192)
    field = line_ref[...]
    for dy in (-1, 0, 1):
        term = lax.dot_general(
            field,
            moved[(1 - dy) * 128 : (1 - dy) * 128 + 1024],
            (((0,), (0,)), ((), ())),
            preferred_element_type=F32,
        )
        for dx in range(3):
            one = term[:, 64 * dx : 64 * dx + 64]
            at = (3 * (dy + 1) + dx) * 256
            sum_ref[at : at + 256, :] = jnp.concatenate([one, one], axis=1)
    owners = part_ref.shape[0]
    each = 2304 // owners
    lane = lax.broadcasted_iota(jnp.int32, (owners, 128), 1)

    def line(j):
        if 2 * j >= each:
            return jnp.zeros((owners, 128), F32)
        even_line = sum_ref[pl.ds(2 * j, owners, stride=each), :]
        odd_line = sum_ref[pl.ds(2 * j + 1, owners, stride=each), :]
        return jnp.where(lane < 64, even_line, odd_line)

    for j in range(5):
        part_ref[:, :, 128 * j : 128 * j + 128] = jnp.stack([line(j), line(j + 5)], axis=1).astype(BF)
def share_kernel(scale, part_ref, turned_ref, share_ref, sems):
    copies = start_all(weight_moves(turned_ref, 9, share_ref, 32), sems)
    total = jnp.sum(part_ref[...].astype(F32), axis=0) * scale
    rows = []
    for j in range(9):
        line = total[j // 5 : j // 5 + 1, 128 * (j % 5) : 128 * (j % 5) + 128]
        rows += [line[:, 0:64], line[:, 64:128]]
    own = jnp.concatenate(rows + [jnp.zeros((14, 64), F32)], axis=0)
    high = own.astype(BF).astype(F32)
    share_ref[0:32, :] = jnp.concatenate([high, own - high], axis=1).astype(BF)
    for copy in copies:
        copy.wait()


def fine_kernel(
    near_ref, sec_ref, late_ref, share_ref, field_ref, one_ref, two_ref,
    out_ref, back_ref, grad_ref,
    weight_ref, tile_ref, in_ref,
):
    row, col = lax.axis_index("rows"), lax.axis_index("cols")
    even = row % 2 == 0
    above, below, _ = near_at(row)
    owned = [share_ref[s, 0:32, :].astype(F32) for s in range(4)]
    grad_ref[...] = jnp.concatenate([(own[:, 0:64] + own[:, 64:128])[0:18] for own in owned], axis=1)
    for s in range(4):
        for n in range(9):
            weight_ref[64 * s : 64 * s + 64, 128 * n : 128 * n + 128] = late_ref[s, 128 + 64 * n : 192 + 64 * n, :]
            weight_ref[64 * s : 64 * s + 64, 1152 + 128 * n : 1280 + 128 * n] = share_ref[
                s, 32 + 64 * n : 96 + 64 * n, :
            ]
    place = lax.broadcasted_iota(jnp.int32, (10, 64, 256), 1)
    framed = ((place >= 16) | (col > 0)) & ((place < 48) | (col < 3))

    def lay_out():
        wide = jnp.where(framed, tile_ref[...].astype(F32), 0.0)
        for at in range(3):
            in_ref[at] = wide[:, 15 + at : 47 + at].astype(BF).reshape(320, 256)

    begin = pl.multiple_of(32 * col, 32)
    before = pl.multiple_of(jnp.maximum(32 * col - 16, 0), 16)
    after = pl.multiple_of(jnp.minimum(32 * col + 32, 112), 16)
    for at, to, size in ((before, 0, 16), (begin, 16, 32), (after, 48, 16)):
        one, two = one_ref[pl.ds(at, size), :], two_ref[pl.ds(at, size), :]
        tile_ref[0, to : to + size, :] = jnp.where(even, two, one)
        tile_ref[9, to : to + size, :] = jnp.where(even, one, two)
    tile_ref[1:9] = field_ref[...]
    lay_out()
    total = jnp.zeros((256, 256), F32)
    for dy in range(3):
        for dx in range(3):
            k = (3 * dy + dx) * 256
            total += lax.dot_general(
                in_ref[dx, 32 * dy : 32 * dy + 256, :],
                weight_ref[:, k : k + 256],
                (((1,), (1,)), ((), ())),
                preferred_element_type=F32,
            )
    out_ref[...] = total.astype(BF)

    left, right = jnp.maximum(col - 1, 0), jnp.minimum(col + 1, 3)
    for tile, at, to, size in ((left, 16, 0, 16), (col, 0, 16, 32), (right, 0, 48, 16)):
        for i, start in ((0, above), (9, below)):
            tile_ref[i, to : to + size, :] = near_ref[tile, pl.ds(start + 32 + at, size), :]
        for i in range(8):
            for half in range(2):
                first = 128 + 256 * half + 32 * i + at
                tile_ref[i + 1, to : to + size, 128 * half : 128 * half + 128] = sec_ref[tile, first : first + size, :]
    lay_out()
    total = jnp.zeros((256, 256), F32)
    for dy in range(3):
        for dx in range(3):
            k = (3 * dy + dx) * 256
            total += jnp.dot(
                in_ref[2 - dx, 32 * (2 - dy) : 32 * (2 - dy) + 256, :],
                weight_ref[:, k : k + 256],
                preferred_element_type=F32,
            )
    back_ref[...] = total.astype(BF)


def on_device(
    fine_noisy, fine_weight, projection, mid_noisy, teacher_weight, student_weight, steps, cotangent
):
    count = lax.axis_size("rows")
    near_pairs = [(i ^ 1, i) for i in range(count)]
    far_pairs = [(i, i + 1 if i % 2 else i - 1) for i in range(1, count - 1)]

    turned = fine_weight.T
    flat = cotangent.reshape(256, 256)
    one, two = call(
        pack_kernel,
        [shape((64, 256), BF), shape((64, 256), BF)],
        [pltpu.SemaphoreType.DMA((6,))],
        MIB,
        56,
        "pack",
        [pl.ANY] * 2,
    )(flat, mid_noisy.reshape(16, 512))
    two = lax.ppermute(two, "rows", far_pairs)
    pairs = [[i, i + 1] for i in range(0, count, 2)]
    one = lax.all_gather(one, "rows", axis=0, tiled=True, axis_index_groups=pairs)
    near = lax.all_gather(jnp.concatenate([one, two, fine_noisy.reshape(256, 256)], axis=0), "cols", axis=0)
    steps = steps.reshape(1, 3)
    sec, middle, base = call(
        first_kernel,
        [shape((896, 128), BF), shape((64, 128), F32), shape((64, 128), F32)],
        [
            pltpu.VMEM((3, 4, 32, 256), BF),
            pltpu.VMEM((192, 512), F32),
            pltpu.VMEM((2, 512), F32),
            pltpu.VMEM((3, 192, 512), BF),
            pltpu.SemaphoreType.DMA((9,)),
        ],
        300 * MIB,
        16,
        "first",
        [pl.ANY] + [pltpu.VMEM] * 3 + [pl.ANY] * 2,
    )(near, teacher_weight, student_weight, steps, flat, projection.T)
    sec = lax.all_gather(sec, "cols", axis=0)
    (late,) = call(
        second_kernel,
        [shape((704, 128), BF)],
        [pltpu.VMEM((3, 128, 512), BF), pltpu.SemaphoreType.DMA((9,))],
        100 * MIB,
        16,
        "second",
        [pltpu.VMEM] * 5 + [pl.ANY],
    )(sec, teacher_weight, middle, base, steps, turned)
    late = lax.all_gather(late, "cols", axis=0)
    part, field, one, two, gap = call(
        grad_kernel,
        [
            shape((count, 2, 640), BF),
            shape((8, 64, 256), BF),
            shape((128, 256), BF),
            shape((128, 256), BF),
            shape((16, 512), BF),
        ],
        [pltpu.VMEM((1024, 256), BF), pltpu.VMEM((2304, 128), F32), pltpu.VMEM((64, 512), F32)],
        1000 * MIB,
        32,
        "grad",
        [pltpu.VMEM] * 3,
    )(near, sec, late)
    part = lax.all_to_all(part, "rows", 0, 0, tiled=True)
    two = lax.ppermute(two, "rows", far_pairs)
    one = lax.ppermute(one, "rows", near_pairs)
    (share,) = call(
        functools.partial(share_kernel, 1.0 / math.sqrt(1024 * count)),
        [shape((608, 128), BF)],
        [pltpu.SemaphoreType.DMA((9,))],
        MIB,
        8,
        "share",
        [pltpu.VMEM, pl.ANY],
    )(part, turned)
    share = lax.all_gather(share, "cols", axis=0)
    share, one, two = lax.optimization_barrier((share, one, two))
    fine_out, grad_input, grad_weight = call(
        fine_kernel,
        [shape((256, 256), BF), shape((256, 256), BF), shape((18, 256), F32)],
        [pltpu.VMEM((256, 2304), BF), pltpu.VMEM((10, 64, 256), BF), pltpu.VMEM((3, 320, 256), BF)],
        1000 * MIB,
        32,
        "fine",
        [pltpu.VMEM] * 7,
    )(near, sec, late, share, field, one, two)
    return (
        fine_out.reshape(8, 32, 256),
        grad_input.reshape(8, 32, 256),
        grad_weight,
        gap.reshape(2, 8, 512),
    )


def solution(mesh):
    placed = (
        P("rows", "cols", None),
        P(None, "cols"),
        P(None, "cols"),
        P("rows", "cols", None),
        P(None, "cols"),
        P(None, "cols"),
        P(),
        P("rows", "cols", None),
    )
    return jax.shard_map(
        on_device,
        mesh=mesh,
        in_specs=placed,
        out_specs=(
            P("rows", "cols", None),
            P("rows", "cols", None),
            P("rows", None),
            P("rows", "cols", None),
        ),
        check_vma=False,
    )
```

```python
import functools
import math

import jax
import jax.numpy as jnp
from jax import lax
from jax.experimental import pallas as pl
from jax.experimental.pallas import tpu as pltpu
from jax.sharding import PartitionSpec as P

BF = jnp.bfloat16
F32 = jnp.float32
MIB = 1024 * 1024


def call(body, outs, scratch, flops, vmem, name, ins, out_spaces=None):
    out_spaces = out_spaces or [pltpu.VMEM] * len(outs)
    return pl.pallas_call(
        body,
        out_shape=outs,
        in_specs=[pl.BlockSpec(memory_space=space) for space in ins],
        out_specs=[pl.BlockSpec(memory_space=space) for space in out_spaces],
        scratch_shapes=scratch,
        compiler_params=pltpu.CompilerParams(vmem_limit_bytes=vmem * MIB),
        cost_estimate=pl.CostEstimate(flops=flops, bytes_accessed=MIB, transcendentals=0),
        name=name,
    )


def shape(dims, kind):
    return jax.ShapeDtypeStruct(dims, kind)


def silu(value):
    return value * (1.0 / (1.0 + jnp.exp(-value)))


def shifted(field, step):
    if step == 0:
        return field
    edge = jnp.zeros((field.shape[0], 1, field.shape[2]), field.dtype)
    if step < 0:
        return jnp.concatenate([edge, field[:, :-1]], axis=1)
    return jnp.concatenate([field[:, 1:], edge], axis=1)


def pack_kernel(cot_ref, mid_ref, one_ref, two_ref, sems):
    even = lax.axis_index("rows") % 2 == 0
    last, first = pl.multiple_of(jnp.where(even, 224, 0), 32), pl.multiple_of(jnp.where(even, 0, 224), 32)
    moves = [
        (mid_ref.at[:, 256 * half : 256 * half + 256], ref.at[16 * half : 16 * half + 16, :])
        for ref in (one_ref, two_ref)
        for half in range(2)
    ]
    moves += [
        (cot_ref.at[pl.ds(last, 32), :], one_ref.at[32:64, :]),
        (cot_ref.at[pl.ds(first, 32), :], two_ref.at[32:64, :]),
    ]
    for copy in start_all(moves, sems):
        copy.wait()


def near_at(row):
    even = row % 2 == 0
    above = pl.multiple_of(jnp.where(even, 128, 0), 64)
    below = pl.multiple_of(jnp.where(even, 64, 128), 64)
    return above, below, pl.multiple_of(jnp.where(even, 0, 64), 64)


def start_all(moves, sems):
    copies = [pltpu.make_async_copy(src, dst, sems.at[n]) for n, (src, dst) in enumerate(moves)]
    for copy in copies:
        copy.start()
    return copies


def waves(angle):
    turns = jnp.round(angle * (0.5 / math.pi))
    rest = (angle - turns * 6.28125) - turns * (2 * math.pi - 6.28125)
    square = rest * rest
    sin, cos = jnp.ones_like(rest), jnp.ones_like(rest)
    for n in range(9, 0, -1):
        cos = 1.0 - square * cos * (1.0 / ((2 * n - 1) * (2 * n)))
        sin = 1.0 - square * sin * (1.0 / ((2 * n) * (2 * n + 1)))
    return rest * sin, cos


def embed(step):
    index = lax.broadcasted_iota(jnp.int32, (1, 256), 1)
    freqs = jnp.ones((1, 256), F32)
    for bit in range(8):
        factor = math.exp(-math.log(10000.0) * 2**bit / 256)
        freqs = jnp.where((index // 2**bit) % 2 == 1, freqs * factor, freqs)
    return jnp.concatenate(waves(step.astype(F32) * freqs), axis=1)


def delta(steps_ref, n):
    return (steps_ref[:, n + 1 : n + 2] - steps_ref[:, n : n + 1]).astype(F32) / 1000.0


def first_kernel(
    near_ref, teacher_ref, steps_ref, cot_ref, proj_ref,
    sec_ref, mid_ref, anchor_ref, lit_ref,
    tile_ref, raw_ref, wave_ref, in_ref, sems,
):
    row, col = lax.axis_index("rows"), lax.axis_index("cols")
    last = lax.axis_size("rows") - 1
    above, below, own = near_at(row)
    moves = [(near_ref.at[:, pl.ds(start, 32), :], tile_ref.at[n]) for n, start in enumerate((above, own, below))]
    moves += [
        (cot_ref.at[:, 128 * n : 128 * n + 128], sec_ref.at[128 + 256 * n : 384 + 256 * n, :]) for n in range(2)
    ]
    moves += [
        (proj_ref.at[:, 128 * n : 128 * n + 128], sec_ref.at[640 + 64 * n : 704 + 64 * n, :]) for n in range(4)
    ]
    copies = start_all(moves, sems)
    for n in range(2):
        wave_ref[n : n + 1, :] = embed(steps_ref[:, n : n + 1])
    lines = []
    for n in range(3):
        copies[n].wait()
        tiles = [tile_ref[n, s].astype(F32) for s in range(4)]
        for half in (0, 8):
            lines.append(
                jnp.concatenate(
                    [jnp.concatenate([t[half : half + 8], t[half + 16 : half + 24]], axis=1) for t in tiles],
                    axis=0,
                )
            )
    raw = jnp.stack(lines)
    raw_ref[...] = raw.reshape(192, 512)
    lit = silu(raw + wave_ref[0:1, :].reshape(1, 1, 512))
    line = lax.broadcasted_iota(jnp.int32, (6, 32, 512), 0)
    inside = ((line >= 2) | (row > 0)) & ((line < 4) | (row < last))
    lit = jnp.where(inside, lit, 0.0)
    for at, step in enumerate((-1, 0, 1)):
        in_ref[at] = shifted(lit, step).astype(BF).reshape(192, 512)
    total = jnp.zeros((128, 128), F32)
    for dy in range(3):
        for dx in range(3):
            k = (3 * dy + dx) * 512
            total += jnp.dot(
                in_ref[dx, 32 * dy : 32 * dy + 128, :], teacher_ref[k : k + 512, :], preferred_element_type=F32
            )
    own = pl.ds(pl.multiple_of(col * 128, 128), 128)
    anchor = raw_ref[32:160, own]
    middle = anchor + delta(steps_ref, 0) * total
    second = silu(middle + wave_ref[1:2, own])
    line = lax.broadcasted_iota(jnp.int32, (128, 128), 0)
    inside = ((line >= 32) | (row > 0)) & ((line < 96) | (row < last))
    sec_ref[0:128, :] = jnp.where(inside, second, 0.0).astype(BF)
    mid_ref[...] = middle[32:96]
    anchor_ref[...] = anchor[32:96]
    lit_ref[...] = in_ref[:, 32:160, :]
    for copy in copies[3:]:
        copy.wait()


EARLY = 5


def weight_moves(turned_ref, lines, out_ref, base):
    return [
        (turned_ref.at[:, 128 * line : 128 * line + 128], out_ref.at[base + 64 * n : base + 64 * n + 64, :])
        for n, line in enumerate(lines)
    ]


def second_kernel(
    sec_ref, teacher_ref, student_ref, mid_ref, anchor_ref, lit_ref, steps_ref, fine_ref, turned_ref, out_ref, in_ref, sems
):
    moves = [
        (fine_ref.at[:, 128 * n : 128 * n + 128], out_ref.at[128 + 256 * n : 384 + 256 * n, :]) for n in range(2)
    ]
    copies = start_all(moves + weight_moves(turned_ref, range(EARLY), out_ref, 640), sems)
    field = jnp.concatenate([sec_ref[s, 0:128, :] for s in range(4)], axis=1).astype(F32).reshape(4, 32, 512)
    for at, step in enumerate((-1, 0, 1)):
        in_ref[at] = shifted(field, step).astype(BF).reshape(128, 512)
    total = jnp.zeros((64, 128), F32)
    for dy in range(3):
        for dx in range(3):
            k = (3 * dy + dx) * 512
            total += jnp.dot(
                in_ref[dx, 32 * dy : 32 * dy + 64, :], teacher_ref[k : k + 512, :], preferred_element_type=F32
            )
    pupil = jnp.zeros((64, 128), F32)
    for dy in range(3):
        for dx in range(3):
            k = (3 * dy + dx) * 512
            pupil += jnp.dot(
                lit_ref[dx, 32 * dy : 32 * dy + 64, :], student_ref[k : k + 512, :], preferred_element_type=F32
            )
    one, two = delta(steps_ref, 0), delta(steps_ref, 1)
    target = mid_ref[...] + two * total
    out_ref[0:64, :] = target.astype(BF)
    out_ref[64:128, :] = (target - (anchor_ref[...] + (one + two) * pupil)).astype(BF)
    for copy in copies:
        copy.wait()


def repeater():
    place = lax.broadcasted_iota(jnp.int32, (128, 32), 0) // 4
    return (place == lax.broadcasted_iota(jnp.int32, (128, 32), 1)).astype(BF)


def lifted(target, proj):
    wide = jnp.dot(repeater(), target, preferred_element_type=F32).astype(BF)
    return lax.dot_general(wide, proj, (((1,), (1,)), ((), ())), preferred_element_type=F32)


def grad_kernel(
    near_ref, sec_ref, late_ref, part_ref, field_ref, one_ref, two_ref, gap_ref, line_ref, sum_ref, gap_scratch
):
    row, col = lax.axis_index("rows"), lax.axis_index("cols")
    above, below, _ = near_at(row)
    even = row % 2 == 0
    pair = pl.multiple_of((col // 2) * 128, 128)
    lanes = pl.ds(pair, 128)
    target = jnp.concatenate([late_ref[s, 0:64, :] for s in range(4)], axis=1)
    proj = jnp.concatenate(
        [
            jnp.concatenate([sec_ref[s, 640 + 64 * n : 704 + 64 * n, :] for n in range(4)], axis=1)
            for s in range(4)
        ],
        axis=0,
    )
    for m in range(2):
        lift = lifted(target[32 * m : 32 * m + 32], proj)
        for i in range(4 * m, 4 * m + 4):
            noisy = jnp.concatenate(
                [
                    jnp.concatenate(
                        [late_ref[s, at + 32 * i : at + 32 * i + 32, :] for at in (128, 384)], axis=1
                    )
                    for s in range(4)
                ],
                axis=0,
            )
            line_ref[128 * i : 128 * i + 128, :] = (noisy.astype(F32) + lift).astype(BF)
    begin = pl.multiple_of(32 * col, 32)
    before = pl.multiple_of(jnp.maximum(32 * col - 16, 0), 16)
    after = pl.multiple_of(jnp.minimum(32 * col + 32, 112), 16)
    for i in range(8):
        for at, to, size in ((before, 0, 16), (begin, 16, 32), (after, 48, 16)):
            field_ref[i, to : to + size, :] = line_ref[pl.ds(128 * i + at, size), :]
    one_ref[...] = jnp.where(even, field_ref[7], field_ref[0])
    two_ref[...] = jnp.where(even, field_ref[0], field_ref[7])
    gap_scratch[...] = jnp.concatenate([late_ref[s, 64:128, :] for s in range(4)], axis=1).astype(F32)
    gap_ref[...] = jnp.concatenate(
        [gap_scratch[pl.ds(pl.multiple_of(32 * i + 8 * col, 8), 8), :] for i in range(2)], axis=0
    ).astype(BF)
    lines = [near_ref[s, pl.ds(above + 32, 32), lanes] for s in range(4)]
    for i in range(8):
        lines += [sec_ref[s, pl.ds(128 + 32 * i + 2 * pair, 32), :] for s in range(4)]
    lines += [near_ref[s, pl.ds(below + 32, 32), lanes] for s in range(4)]
    cot = jnp.concatenate(lines, axis=0).astype(F32)
    cot = jnp.where(col % 2 == 1, cot[:, 64:128], cot[:, 0:64]).reshape(10, 128, 64)
    moved = jnp.concatenate([shifted(cot, -dx) for dx in (-1, 0, 1)], axis=2).astype(BF).reshape(1280, 192)
    field = line_ref[...].T
    for dy in (-1, 0, 1):
        term = jnp.dot(field, moved[(1 - dy) * 128 : (1 - dy) * 128 + 1024], preferred_element_type=F32)
        for dx in range(3):
            one = term[:, 64 * dx : 64 * dx + 64]
            at = (3 * (dy + 1) + dx) * 256
            sum_ref[at : at + 256, :] = jnp.concatenate([one, one], axis=1)
    owners = part_ref.shape[0]
    each = 2304 // owners
    lane = lax.broadcasted_iota(jnp.int32, (owners, 128), 1)

    def line(j):
        if 2 * j >= each:
            return jnp.zeros((owners, 128), F32)
        even_line = sum_ref[pl.ds(2 * j, owners, stride=each), :]
        odd_line = sum_ref[pl.ds(2 * j + 1, owners, stride=each), :]
        return jnp.where(lane < 64, even_line, odd_line)

    for j in range(5):
        part_ref[:, :, 128 * j : 128 * j + 128] = jnp.stack([line(j), line(j + 5)], axis=1).astype(BF)
def share_kernel(scale, part_ref, turned_ref, share_ref, sems):
    copies = start_all(weight_moves(turned_ref, range(EARLY, 18), share_ref, 32), sems)
    total = jnp.sum(part_ref[...].astype(F32), axis=0) * scale
    rows = []
    for j in range(9):
        line = total[j // 5 : j // 5 + 1, 128 * (j % 5) : 128 * (j % 5) + 128]
        rows += [line[:, 0:64], line[:, 64:128]]
    own = jnp.concatenate(rows + [jnp.zeros((14, 64), F32)], axis=0)
    high = own.astype(BF).astype(F32)
    share_ref[0:32, :] = jnp.concatenate([high, own - high], axis=1).astype(BF)
    for copy in copies:
        copy.wait()


def fine_kernel(
    near_ref, sec_ref, late_ref, share_ref, field_ref, one_ref, two_ref,
    out_ref, back_ref, grad_ref,
    weight_ref, tile_ref, in_ref,
):
    row, col = lax.axis_index("rows"), lax.axis_index("cols")
    even = row % 2 == 0
    above, below, _ = near_at(row)
    owned = [share_ref[s, 0:32, :].astype(F32) for s in range(4)]
    grad_ref[...] = jnp.concatenate([(own[:, 0:64] + own[:, 64:128])[0:18] for own in owned], axis=1)
    for s in range(4):
        for n in range(18):
            ref, at = (late_ref, 640 + 64 * n) if n < EARLY else (share_ref, 32 + 64 * (n - EARLY))
            weight_ref[64 * s : 64 * s + 64, 128 * n : 128 * n + 128] = ref[s, at : at + 64, :]
    place = lax.broadcasted_iota(jnp.int32, (10, 64, 256), 1)
    framed = ((place >= 16) | (col > 0)) & ((place < 48) | (col < 3))

    def lay_out():
        wide = jnp.where(framed, tile_ref[...].astype(F32), 0.0)
        for at in range(3):
            in_ref[at] = wide[:, 15 + at : 47 + at].astype(BF).reshape(320, 256)

    one, two = one_ref[...], two_ref[...]
    tile_ref[0] = jnp.where(even, two, one)
    tile_ref[9] = jnp.where(even, one, two)
    tile_ref[1:9] = field_ref[...]
    lay_out()
    total = jnp.zeros((256, 256), F32)
    for dy in range(3):
        for dx in range(3):
            k = (3 * dy + dx) * 256
            total += lax.dot_general(
                in_ref[dx, 32 * dy : 32 * dy + 256, :],
                weight_ref[:, k : k + 256],
                (((1,), (1,)), ((), ())),
                preferred_element_type=F32,
            )
    out_ref[...] = total.astype(BF)

    left, right = jnp.maximum(col - 1, 0), jnp.minimum(col + 1, 3)
    for tile, at, to, size in ((left, 16, 0, 16), (col, 0, 16, 32), (right, 0, 48, 16)):
        for i, start in ((0, above), (9, below)):
            tile_ref[i, to : to + size, :] = near_ref[tile, pl.ds(start + 32 + at, size), :]
        for i in range(8):
            for half in range(2):
                first = 128 + 256 * half + 32 * i + at
                tile_ref[i + 1, to : to + size, 128 * half : 128 * half + 128] = sec_ref[tile, first : first + size, :]
    lay_out()
    total = jnp.zeros((256, 256), F32)
    for dy in range(3):
        for dx in range(3):
            k = (3 * dy + dx) * 256
            total += jnp.dot(
                in_ref[2 - dx, 32 * (2 - dy) : 32 * (2 - dy) + 256, :],
                weight_ref[:, k : k + 256],
                preferred_element_type=F32,
            )
    back_ref[...] = total.astype(BF)


def on_device(
    fine_noisy, fine_weight, projection, mid_noisy, teacher_weight, student_weight, steps, cotangent
):
    count = lax.axis_size("rows")
    near_pairs = [(i ^ 1, i) for i in range(count)]
    far_pairs = [(i, i + 1 if i % 2 else i - 1) for i in range(1, count - 1)]

    turned = fine_weight.T
    flat = cotangent.reshape(256, 256)
    one, two = call(
        pack_kernel,
        [shape((64, 256), BF), shape((64, 256), BF)],
        [pltpu.SemaphoreType.DMA((6,))],
        20000 * MIB,
        56,
        "pack",
        [pl.ANY] * 2,
    )(flat, mid_noisy.reshape(16, 512))
    two = lax.ppermute(two, "rows", far_pairs)
    pairs = [[i, i + 1] for i in range(0, count, 2)]
    one = lax.all_gather(one, "rows", axis=0, tiled=True, axis_index_groups=pairs)
    near = lax.all_gather(jnp.concatenate([one, two], axis=0), "cols", axis=0)
    steps = steps.reshape(1, 3)
    sec, middle, anchor, lit = call(
        first_kernel,
        [shape((896, 128), BF), shape((64, 128), F32), shape((64, 128), F32), shape((3, 128, 512), BF)],
        [
            pltpu.VMEM((3, 4, 32, 256), BF),
            pltpu.VMEM((192, 512), F32),
            pltpu.VMEM((2, 512), F32),
            pltpu.VMEM((3, 192, 512), BF),
            pltpu.SemaphoreType.DMA((9,)),
        ],
        300 * MIB,
        16,
        "first",
        [pl.ANY] + [pltpu.VMEM] * 2 + [pl.ANY] * 2,
    )(near, teacher_weight, steps, flat, projection.T)
    sec = lax.all_gather(sec, "cols", axis=0)
    (late,) = call(
        second_kernel,
        [shape((640 + 64 * EARLY, 128), BF)],
        [pltpu.VMEM((3, 128, 512), BF), pltpu.SemaphoreType.DMA((2 + EARLY,))],
        100 * MIB,
        16,
        "second",
        [pltpu.VMEM] * 7 + [pl.ANY] * 2,
    )(sec, teacher_weight, student_weight, middle, anchor, lit, steps, fine_noisy.reshape(256, 256), turned)
    late = lax.all_gather(late, "cols", axis=0)
    part, field, one, two, gap = call(
        grad_kernel,
        [
            shape((count, 2, 640), BF),
            shape((8, 64, 256), BF),
            shape((64, 256), BF),
            shape((64, 256), BF),
            shape((16, 512), BF),
        ],
        [pltpu.VMEM((1024, 256), BF), pltpu.VMEM((2304, 128), F32), pltpu.VMEM((64, 512), F32)],
        1000 * MIB,
        32,
        "grad",
        [pltpu.VMEM] * 3,
    )(near, sec, late)
    part = lax.all_to_all(part, "rows", 0, 0, tiled=True)
    two = lax.ppermute(two, "rows", far_pairs)
    one = lax.ppermute(one, "rows", near_pairs)
    (share,) = call(
        functools.partial(share_kernel, 1.0 / math.sqrt(1024 * count)),
        [shape((32 + 64 * (18 - EARLY), 128), BF)],
        [pltpu.SemaphoreType.DMA((18 - EARLY,))],
        MIB,
        8,
        "share",
        [pltpu.VMEM, pl.ANY],
    )(part, turned)
    share = lax.all_gather(share, "cols", axis=0)
    share, one, two = lax.optimization_barrier((share, one, two))
    fine_out, grad_input, grad_weight = call(
        fine_kernel,
        [shape((256, 256), BF), shape((256, 256), BF), shape((18, 256), F32)],
        [pltpu.VMEM((256, 2304), BF), pltpu.VMEM((10, 64, 256), BF), pltpu.VMEM((3, 320, 256), BF)],
        1000 * MIB,
        32,
        "fine",
        [pltpu.VMEM] * 7,
    )(near, sec, late, share, field, one, two)
    return (
        fine_out.reshape(8, 32, 256),
        grad_input.reshape(8, 32, 256),
        grad_weight,
        gap.reshape(2, 8, 512),
    )


def solution(mesh):
    placed = (
        P("rows", "cols", None),
        P(None, "cols"),
        P(None, "cols"),
        P("rows", "cols", None),
        P(None, "cols"),
        P(None, "cols"),
        P(),
        P("rows", "cols", None),
    )
    return jax.shard_map(
        on_device,
        mesh=mesh,
        in_specs=placed,
        out_specs=(
            P("rows", "cols", None),
            P("rows", "cols", None),
            P("rows", None),
            P("rows", "cols", None),
        ),
        check_vma=False,
    )
```

```python
import functools
import math

import jax
import jax.numpy as jnp
from jax import lax
from jax.experimental import pallas as pl
from jax.experimental.pallas import tpu as pltpu
from jax.sharding import PartitionSpec as P

BF = jnp.bfloat16
F32 = jnp.float32
MIB = 1024 * 1024


def call(body, outs, scratch, flops, vmem, name, ins, out_spaces=None):
    out_spaces = out_spaces or [pltpu.VMEM] * len(outs)
    return pl.pallas_call(
        body,
        out_shape=outs,
        in_specs=[pl.BlockSpec(memory_space=space) for space in ins],
        out_specs=[pl.BlockSpec(memory_space=space) for space in out_spaces],
        scratch_shapes=scratch,
        compiler_params=pltpu.CompilerParams(vmem_limit_bytes=vmem * MIB),
        cost_estimate=pl.CostEstimate(flops=flops, bytes_accessed=MIB, transcendentals=0),
        name=name,
    )


def shape(dims, kind):
    return jax.ShapeDtypeStruct(dims, kind)


def silu(value):
    return value * (1.0 / (1.0 + jnp.exp(-value)))


def shifted(field, step):
    if step == 0:
        return field
    edge = jnp.zeros((field.shape[0], 1, field.shape[2]), field.dtype)
    if step < 0:
        return jnp.concatenate([edge, field[:, :-1]], axis=1)
    return jnp.concatenate([field[:, 1:], edge], axis=1)


def pack_kernel(cot_ref, mid_ref, one_ref, two_ref, sems):
    even = lax.axis_index("rows") % 2 == 0
    last, first = pl.multiple_of(jnp.where(even, 224, 0), 32), pl.multiple_of(jnp.where(even, 0, 224), 32)
    moves = [
        (mid_ref.at[:, 256 * half : 256 * half + 256], ref.at[16 * half : 16 * half + 16, :])
        for ref in (one_ref, two_ref)
        for half in range(2)
    ]
    moves += [
        (cot_ref.at[pl.ds(last, 32), :], one_ref.at[32:64, :]),
        (cot_ref.at[pl.ds(first, 32), :], two_ref.at[32:64, :]),
    ]
    for copy in start_all(moves, sems):
        copy.wait()


def near_at(row):
    even = row % 2 == 0
    above = pl.multiple_of(jnp.where(even, 128, 0), 64)
    below = pl.multiple_of(jnp.where(even, 64, 128), 64)
    return above, below, pl.multiple_of(jnp.where(even, 0, 64), 64)


def start_all(moves, sems):
    copies = [pltpu.make_async_copy(src, dst, sems.at[n]) for n, (src, dst) in enumerate(moves)]
    for copy in copies:
        copy.start()
    return copies


def waves(angle):
    turns = jnp.round(angle * (0.5 / math.pi))
    rest = (angle - turns * 6.28125) - turns * (2 * math.pi - 6.28125)
    square = rest * rest
    sin, cos = jnp.ones_like(rest), jnp.ones_like(rest)
    for n in range(9, 0, -1):
        cos = 1.0 - square * cos * (1.0 / ((2 * n - 1) * (2 * n)))
        sin = 1.0 - square * sin * (1.0 / ((2 * n) * (2 * n + 1)))
    return rest * sin, cos


def embed(step):
    index = lax.broadcasted_iota(jnp.int32, (1, 256), 1)
    freqs = jnp.ones((1, 256), F32)
    for bit in range(8):
        factor = math.exp(-math.log(10000.0) * 2**bit / 256)
        freqs = jnp.where((index // 2**bit) % 2 == 1, freqs * factor, freqs)
    return jnp.concatenate(waves(step.astype(F32) * freqs), axis=1)


def delta(steps_ref, n):
    return (steps_ref[:, n + 1 : n + 2] - steps_ref[:, n : n + 1]).astype(F32) / 1000.0


def first_kernel(
    near_ref, teacher_ref, steps_ref, cot_ref, proj_ref,
    sec_ref, mid_ref, anchor_ref, lit_ref,
    tile_ref, raw_ref, wave_ref, in_ref, sems,
):
    row, col = lax.axis_index("rows"), lax.axis_index("cols")
    last = lax.axis_size("rows") - 1
    above, below, own = near_at(row)
    moves = [(near_ref.at[:, pl.ds(start, 32), :], tile_ref.at[n]) for n, start in enumerate((above, own, below))]
    moves += [
        (cot_ref.at[:, 128 * n : 128 * n + 128], sec_ref.at[128 + 256 * n : 384 + 256 * n, :]) for n in range(2)
    ]
    moves += [
        (proj_ref.at[:, 128 * n : 128 * n + 128], sec_ref.at[640 + 64 * n : 704 + 64 * n, :]) for n in range(4)
    ]
    copies = start_all(moves, sems)
    for n in range(2):
        wave_ref[n : n + 1, :] = embed(steps_ref[:, n : n + 1])
    lines = []
    for n in range(3):
        copies[n].wait()
        tiles = [tile_ref[n, s].astype(F32) for s in range(4)]
        for half in (0, 8):
            lines.append(
                jnp.concatenate(
                    [jnp.concatenate([t[half : half + 8], t[half + 16 : half + 24]], axis=1) for t in tiles],
                    axis=0,
                )
            )
    raw = jnp.stack(lines)
    raw_ref[...] = raw.reshape(192, 512)
    lit = silu(raw + wave_ref[0:1, :].reshape(1, 1, 512))
    line = lax.broadcasted_iota(jnp.int32, (6, 32, 512), 0)
    inside = ((line >= 2) | (row > 0)) & ((line < 4) | (row < last))
    lit = jnp.where(inside, lit, 0.0)
    for at, step in enumerate((-1, 0, 1)):
        in_ref[at] = shifted(lit, step).astype(BF).reshape(192, 512)
    total = jnp.zeros((128, 128), F32)
    for dy in range(3):
        for dx in range(3):
            k = (3 * dy + dx) * 512
            total += jnp.dot(
                in_ref[dx, 32 * dy : 32 * dy + 128, :], teacher_ref[k : k + 512, :], preferred_element_type=F32
            )
    own = pl.ds(pl.multiple_of(col * 128, 128), 128)
    anchor = raw_ref[32:160, own]
    middle = anchor + delta(steps_ref, 0) * total
    second = silu(middle + wave_ref[1:2, own])
    line = lax.broadcasted_iota(jnp.int32, (128, 128), 0)
    inside = ((line >= 32) | (row > 0)) & ((line < 96) | (row < last))
    sec_ref[0:128, :] = jnp.where(inside, second, 0.0).astype(BF)
    mid_ref[...] = middle[32:96]
    anchor_ref[...] = anchor[32:96]
    lit_ref[...] = in_ref[:, 32:160, :]
    for copy in copies[3:]:
        copy.wait()


def second_kernel(
    sec_ref, teacher_ref, student_ref, mid_ref, anchor_ref, lit_ref, steps_ref, fine_ref, out_ref, in_ref, sems
):
    moves = [
        (fine_ref.at[:, 128 * n : 128 * n + 128], out_ref.at[128 + 256 * n : 384 + 256 * n, :]) for n in range(2)
    ]
    copies = start_all(moves, sems)
    field = jnp.concatenate([sec_ref[s, 0:128, :] for s in range(4)], axis=1).astype(F32).reshape(4, 32, 512)
    for at, step in enumerate((-1, 0, 1)):
        in_ref[at] = shifted(field, step).astype(BF).reshape(128, 512)
    total = jnp.zeros((64, 128), F32)
    for dy in range(3):
        for dx in range(3):
            k = (3 * dy + dx) * 512
            total += jnp.dot(
                in_ref[dx, 32 * dy : 32 * dy + 64, :], teacher_ref[k : k + 512, :], preferred_element_type=F32
            )
    pupil = jnp.zeros((64, 128), F32)
    for dy in range(3):
        for dx in range(3):
            k = (3 * dy + dx) * 512
            pupil += jnp.dot(
                lit_ref[dx, 32 * dy : 32 * dy + 64, :], student_ref[k : k + 512, :], preferred_element_type=F32
            )
    one, two = delta(steps_ref, 0), delta(steps_ref, 1)
    target = mid_ref[...] + two * total
    out_ref[0:64, :] = target.astype(BF)
    out_ref[64:128, :] = (target - (anchor_ref[...] + (one + two) * pupil)).astype(BF)
    for copy in copies:
        copy.wait()


def repeater():
    place = lax.broadcasted_iota(jnp.int32, (128, 32), 0) // 4
    return (place == lax.broadcasted_iota(jnp.int32, (128, 32), 1)).astype(BF)


def lifted(target, proj):
    wide = jnp.dot(repeater(), target, preferred_element_type=F32).astype(BF)
    return lax.dot_general(wide, proj, (((1,), (1,)), ((), ())), preferred_element_type=F32)


def grad_kernel(
    near_ref, sec_ref, late_ref, part_ref, field_ref, one_ref, two_ref, gap_ref, line_ref, sum_ref, gap_scratch
):
    row, col = lax.axis_index("rows"), lax.axis_index("cols")
    above, below, _ = near_at(row)
    even = row % 2 == 0
    pair = pl.multiple_of((col // 2) * 128, 128)
    lanes = pl.ds(pair, 128)
    target = jnp.concatenate([late_ref[s, 0:64, :] for s in range(4)], axis=1)
    proj = jnp.concatenate(
        [
            jnp.concatenate([sec_ref[s, 640 + 64 * n : 704 + 64 * n, :] for n in range(4)], axis=1)
            for s in range(4)
        ],
        axis=0,
    )
    for m in range(2):
        lift = lifted(target[32 * m : 32 * m + 32], proj)
        for i in range(4 * m, 4 * m + 4):
            noisy = jnp.concatenate(
                [
                    jnp.concatenate(
                        [late_ref[s, at + 32 * i : at + 32 * i + 32, :] for at in (128, 384)], axis=1
                    )
                    for s in range(4)
                ],
                axis=0,
            )
            line_ref[128 * i : 128 * i + 128, :] = (noisy.astype(F32) + lift).astype(BF)
    begin = pl.multiple_of(32 * col, 32)
    before = pl.multiple_of(jnp.maximum(32 * col - 16, 0), 16)
    after = pl.multiple_of(jnp.minimum(32 * col + 32, 112), 16)
    for i in range(8):
        for at, to, size in ((before, 0, 16), (begin, 16, 32), (after, 48, 16)):
            field_ref[i, to : to + size, :] = line_ref[pl.ds(128 * i + at, size), :]
    one_ref[...] = jnp.where(even, field_ref[7], field_ref[0])
    two_ref[...] = jnp.where(even, field_ref[0], field_ref[7])
    gap_scratch[...] = jnp.concatenate([late_ref[s, 64:128, :] for s in range(4)], axis=1).astype(F32)
    gap_ref[...] = jnp.concatenate(
        [gap_scratch[pl.ds(pl.multiple_of(32 * i + 8 * col, 8), 8), :] for i in range(2)], axis=0
    ).astype(BF)
    lines = [near_ref[s, pl.ds(above + 32, 32), lanes] for s in range(4)]
    for i in range(8):
        lines += [sec_ref[s, pl.ds(128 + 32 * i + 2 * pair, 32), :] for s in range(4)]
    lines += [near_ref[s, pl.ds(below + 32, 32), lanes] for s in range(4)]
    cot = jnp.concatenate(lines, axis=0).astype(F32)
    cot = jnp.where(col % 2 == 1, cot[:, 64:128], cot[:, 0:64]).reshape(10, 128, 64)
    moved = jnp.concatenate([shifted(cot, -dx) for dx in (-1, 0, 1)], axis=2).astype(BF).reshape(1280, 192)
    field = line_ref[...].T
    for dy in (-1, 0, 1):
        term = jnp.dot(field, moved[(1 - dy) * 128 : (1 - dy) * 128 + 1024], preferred_element_type=F32)
        for dx in range(3):
            one = term[:, 64 * dx : 64 * dx + 64]
            at = (3 * (dy + 1) + dx) * 256
            sum_ref[at : at + 256, :] = jnp.concatenate([one, one], axis=1)
    owners = part_ref.shape[0]
    each = 2304 // owners
    lane = lax.broadcasted_iota(jnp.int32, (owners, 128), 1)

    def line(j):
        if 2 * j >= each:
            return jnp.zeros((owners, 128), F32)
        even_line = sum_ref[pl.ds(2 * j, owners, stride=each), :]
        odd_line = sum_ref[pl.ds(2 * j + 1, owners, stride=each), :]
        return jnp.where(lane < 64, even_line, odd_line)

    for j in range(5):
        part_ref[:, :, 128 * j : 128 * j + 128] = jnp.stack([line(j), line(j + 5)], axis=1).astype(BF)
def share_kernel(scale, part_ref, share_ref):
    total = jnp.sum(part_ref[...].astype(F32), axis=0) * scale
    rows = []
    for j in range(9):
        line = total[j // 5 : j // 5 + 1, 128 * (j % 5) : 128 * (j % 5) + 128]
        rows += [line[:, 0:64], line[:, 64:128]]
    own = jnp.concatenate(rows + [jnp.zeros((14, 64), F32)], axis=0)
    high = own.astype(BF).astype(F32)
    share_ref[...] = jnp.concatenate([high, own - high], axis=1).astype(BF)


def fine_kernel(
    near_ref, sec_ref, turned_ref, beside_ref, across_ref, corner_ref, share_ref, field_ref, one_ref, two_ref,
    out_ref, back_ref, grad_ref,
    weight_ref, tile_ref, in_ref,
):
    row, col = lax.axis_index("rows"), lax.axis_index("cols")
    even = row % 2 == 0
    above, below, _ = near_at(row)
    owned = [share_ref[s, 0:32, :].astype(F32) for s in range(4)]
    grad_ref[...] = jnp.concatenate([(own[:, 0:64] + own[:, 64:128])[0:18] for own in owned], axis=1)
    for k, block in enumerate((turned_ref, beside_ref, across_ref, corner_ref)):
        tile = jnp.bitwise_xor(col, k)
        weight_ref[pl.ds(pl.multiple_of(64 * tile, 64), 64), :] = block[...]
    place = lax.broadcasted_iota(jnp.int32, (10, 64, 256), 1)
    framed = ((place >= 16) | (col > 0)) & ((place < 48) | (col < 3))

    def lay_out():
        wide = jnp.where(framed, tile_ref[...].astype(F32), 0.0)
        for at in range(3):
            in_ref[at] = wide[:, 15 + at : 47 + at].astype(BF).reshape(320, 256)

    one, two = one_ref[...], two_ref[...]
    tile_ref[0] = jnp.where(even, two, one)
    tile_ref[9] = jnp.where(even, one, two)
    tile_ref[1:9] = field_ref[...]
    lay_out()
    total = jnp.zeros((256, 256), F32)
    for dy in range(3):
        for dx in range(3):
            k = (3 * dy + dx) * 256
            total += lax.dot_general(
                in_ref[dx, 32 * dy : 32 * dy + 256, :],
                weight_ref[:, k : k + 256],
                (((1,), (1,)), ((), ())),
                preferred_element_type=F32,
            )
    out_ref[...] = total.astype(BF)

    left, right = jnp.maximum(col - 1, 0), jnp.minimum(col + 1, 3)
    for tile, at, to, size in ((left, 16, 0, 16), (col, 0, 16, 32), (right, 0, 48, 16)):
        for i, start in ((0, above), (9, below)):
            tile_ref[i, to : to + size, :] = near_ref[tile, pl.ds(start + 32 + at, size), :]
        for i in range(8):
            for half in range(2):
                first = 128 + 256 * half + 32 * i + at
                tile_ref[i + 1, to : to + size, 128 * half : 128 * half + 128] = sec_ref[tile, first : first + size, :]
    lay_out()
    total = jnp.zeros((256, 256), F32)
    for dy in range(3):
        for dx in range(3):
            k = (3 * dy + dx) * 256
            total += jnp.dot(
                in_ref[2 - dx, 32 * (2 - dy) : 32 * (2 - dy) + 256, :],
                weight_ref[:, k : k + 256],
                preferred_element_type=F32,
            )
    back_ref[...] = total.astype(BF)


def on_device(
    fine_noisy, fine_weight, projection, mid_noisy, teacher_weight, student_weight, steps, cotangent
):
    count = lax.axis_size("rows")
    near_pairs = [(i ^ 1, i) for i in range(count)]
    far_pairs = [(i, i + 1 if i % 2 else i - 1) for i in range(1, count - 1)]

    flat = cotangent.reshape(256, 256)
    one, two = call(
        pack_kernel,
        [shape((64, 256), BF), shape((64, 256), BF)],
        [pltpu.SemaphoreType.DMA((6,))],
        20000 * MIB,
        56,
        "pack",
        [pl.ANY] * 2,
    )(flat, mid_noisy.reshape(16, 512))
    two = lax.ppermute(two, "rows", far_pairs)
    pairs = [[i, i + 1] for i in range(0, count, 2)]
    one = lax.all_gather(one, "rows", axis=0, tiled=True, axis_index_groups=pairs)
    near = lax.all_gather(jnp.concatenate([one, two], axis=0), "cols", axis=0)
    steps = steps.reshape(1, 3)
    sec, middle, anchor, lit = call(
        first_kernel,
        [shape((896, 128), BF), shape((64, 128), F32), shape((64, 128), F32), shape((3, 128, 512), BF)],
        [
            pltpu.VMEM((3, 4, 32, 256), BF),
            pltpu.VMEM((192, 512), F32),
            pltpu.VMEM((2, 512), F32),
            pltpu.VMEM((3, 192, 512), BF),
            pltpu.SemaphoreType.DMA((9,)),
        ],
        300 * MIB,
        16,
        "first",
        [pl.ANY] + [pltpu.VMEM] * 2 + [pl.ANY] * 2,
    )(near, teacher_weight, steps, flat, projection.T)
    sec = lax.all_gather(sec, "cols", axis=0)
    (late,) = call(
        second_kernel,
        [shape((640, 128), BF)],
        [pltpu.VMEM((3, 128, 512), BF), pltpu.SemaphoreType.DMA((2,))],
        100 * MIB,
        16,
        "second",
        [pltpu.VMEM] * 7 + [pl.ANY],
    )(sec, teacher_weight, student_weight, middle, anchor, lit, steps, fine_noisy.reshape(256, 256))
    late = lax.all_gather(late, "cols", axis=0)
    part, field, one, two, gap = call(
        grad_kernel,
        [
            shape((count, 2, 640), BF),
            shape((8, 64, 256), BF),
            shape((64, 256), BF),
            shape((64, 256), BF),
            shape((16, 512), BF),
        ],
        [pltpu.VMEM((1024, 256), BF), pltpu.VMEM((2304, 128), F32), pltpu.VMEM((64, 512), F32)],
        1000 * MIB,
        32,
        "grad",
        [pltpu.VMEM] * 3,
    )(near, sec, late)
    turned, one, two, part = lax.optimization_barrier((fine_weight.T, one, two, part))
    part = lax.all_to_all(part, "rows", 0, 0, tiled=True)
    across = lax.ppermute(turned, "cols", [(i, i ^ 2) for i in range(4)])
    beside = lax.ppermute(turned, "cols", [(i, i ^ 1) for i in range(4)])
    two = lax.ppermute(two, "rows", far_pairs)
    one = lax.ppermute(one, "rows", near_pairs)
    across, one, two = lax.optimization_barrier((across, one, two))
    corner = lax.ppermute(across, "cols", [(i, i ^ 1) for i in range(4)])
    (share,) = call(
        functools.partial(share_kernel, 1.0 / math.sqrt(1024 * count)),
        [shape((32, 128), BF)],
        [],
        MIB,
        8,
        "share",
        [pltpu.VMEM],
    )(part)
    share = lax.all_gather(share, "cols", axis=0)
    share, one, two = lax.optimization_barrier((share, one, two))
    fine_out, grad_input, grad_weight = call(
        fine_kernel,
        [shape((256, 256), BF), shape((256, 256), BF), shape((18, 256), F32)],
        [pltpu.VMEM((256, 2304), BF), pltpu.VMEM((10, 64, 256), BF), pltpu.VMEM((3, 320, 256), BF)],
        1000 * MIB,
        32,
        "fine",
        [pltpu.VMEM] * 10,
    )(near, sec, turned, beside, across, corner, share, field, one, two)
    return (
        fine_out.reshape(8, 32, 256),
        grad_input.reshape(8, 32, 256),
        grad_weight,
        gap.reshape(2, 8, 512),
    )


def solution(mesh):
    placed = (
        P("rows", "cols", None),
        P(None, "cols"),
        P(None, "cols"),
        P("rows", "cols", None),
        P(None, "cols"),
        P(None, "cols"),
        P(),
        P("rows", "cols", None),
    )
    return jax.shard_map(
        on_device,
        mesh=mesh,
        in_specs=placed,
        out_specs=(
            P("rows", "cols", None),
            P("rows", "cols", None),
            P("rows", None),
            P("rows", "cols", None),
        ),
        check_vma=False,
    )
```

```python
import functools
import math

import jax
import jax.numpy as jnp
from jax import lax
from jax.experimental import pallas as pl
from jax.experimental.pallas import tpu as pltpu
from jax.sharding import PartitionSpec as P

BF = jnp.bfloat16
F32 = jnp.float32
MIB = 1024 * 1024


def call(body, outs, scratch, flops, vmem, name, ins, out_spaces=None):
    out_spaces = out_spaces or [pltpu.VMEM] * len(outs)
    return pl.pallas_call(
        body,
        out_shape=outs,
        in_specs=[pl.BlockSpec(memory_space=space) for space in ins],
        out_specs=[pl.BlockSpec(memory_space=space) for space in out_spaces],
        scratch_shapes=scratch,
        compiler_params=pltpu.CompilerParams(vmem_limit_bytes=vmem * MIB),
        cost_estimate=pl.CostEstimate(flops=flops, bytes_accessed=MIB, transcendentals=0),
        name=name,
    )


def shape(dims, kind):
    return jax.ShapeDtypeStruct(dims, kind)


def silu(value):
    return value * (1.0 / (1.0 + jnp.exp(-value)))


def shifted(field, step):
    if step == 0:
        return field
    edge = jnp.zeros((field.shape[0], 1, field.shape[2]), field.dtype)
    if step < 0:
        return jnp.concatenate([edge, field[:, :-1]], axis=1)
    return jnp.concatenate([field[:, 1:], edge], axis=1)


def pack_kernel(cot_ref, mid_ref, one_ref, two_ref, sems):
    even = lax.axis_index("rows") % 2 == 0
    last, first = pl.multiple_of(jnp.where(even, 224, 0), 32), pl.multiple_of(jnp.where(even, 0, 224), 32)
    moves = [
        (mid_ref.at[:, 256 * half : 256 * half + 256], ref.at[16 * half : 16 * half + 16, :])
        for ref in (one_ref, two_ref)
        for half in range(2)
    ]
    moves += [
        (cot_ref.at[pl.ds(last, 32), :], one_ref.at[32:64, :]),
        (cot_ref.at[pl.ds(first, 32), :], two_ref.at[32:64, :]),
    ]
    for copy in start_all(moves, sems):
        copy.wait()


def near_at(row):
    even = row % 2 == 0
    above = pl.multiple_of(jnp.where(even, 128, 0), 64)
    below = pl.multiple_of(jnp.where(even, 64, 128), 64)
    return above, below, pl.multiple_of(jnp.where(even, 0, 64), 64)


def start_all(moves, sems):
    copies = [pltpu.make_async_copy(src, dst, sems.at[n]) for n, (src, dst) in enumerate(moves)]
    for copy in copies:
        copy.start()
    return copies


def waves(angle):
    turns = jnp.round(angle * (0.5 / math.pi))
    rest = (angle - turns * 6.28125) - turns * (2 * math.pi - 6.28125)
    square = rest * rest
    sin, cos = jnp.ones_like(rest), jnp.ones_like(rest)
    for n in range(9, 0, -1):
        cos = 1.0 - square * cos * (1.0 / ((2 * n - 1) * (2 * n)))
        sin = 1.0 - square * sin * (1.0 / ((2 * n) * (2 * n + 1)))
    return rest * sin, cos


def embed(step):
    index = lax.broadcasted_iota(jnp.int32, (1, 256), 1)
    freqs = jnp.ones((1, 256), F32)
    for bit in range(8):
        factor = math.exp(-math.log(10000.0) * 2**bit / 256)
        freqs = jnp.where((index // 2**bit) % 2 == 1, freqs * factor, freqs)
    return jnp.concatenate(waves(step.astype(F32) * freqs), axis=1)


def delta(steps_ref, n):
    return (steps_ref[:, n + 1 : n + 2] - steps_ref[:, n : n + 1]).astype(F32) / 1000.0


def first_kernel(
    near_ref, teacher_ref, steps_ref, cot_ref, proj_ref,
    sec_ref, mid_ref, anchor_ref, lit_ref,
    tile_ref, raw_ref, wave_ref, in_ref, sems,
):
    row, col = lax.axis_index("rows"), lax.axis_index("cols")
    last = lax.axis_size("rows") - 1
    above, below, own = near_at(row)
    moves = [(near_ref.at[:, pl.ds(start, 32), :], tile_ref.at[n]) for n, start in enumerate((above, own, below))]
    moves += [
        (cot_ref.at[:, 128 * n : 128 * n + 128], sec_ref.at[128 + 256 * n : 384 + 256 * n, :]) for n in range(2)
    ]
    moves += [
        (proj_ref.at[:, 128 * n : 128 * n + 128], sec_ref.at[640 + 64 * n : 704 + 64 * n, :]) for n in range(4)
    ]
    copies = start_all(moves, sems)
    for n in range(2):
        wave_ref[n : n + 1, :] = embed(steps_ref[:, n : n + 1])
    lines = []
    for n in range(3):
        copies[n].wait()
        tiles = [tile_ref[n, s].astype(F32) for s in range(4)]
        for half in (0, 8):
            lines.append(
                jnp.concatenate(
                    [jnp.concatenate([t[half : half + 8], t[half + 16 : half + 24]], axis=1) for t in tiles],
                    axis=0,
                )
            )
    raw = jnp.stack(lines)
    raw_ref[...] = raw.reshape(192, 512)
    lit = silu(raw + wave_ref[0:1, :].reshape(1, 1, 512))
    line = lax.broadcasted_iota(jnp.int32, (6, 32, 512), 0)
    inside = ((line >= 2) | (row > 0)) & ((line < 4) | (row < last))
    lit = jnp.where(inside, lit, 0.0)
    for at, step in enumerate((-1, 0, 1)):
        in_ref[at] = shifted(lit, step).astype(BF).reshape(192, 512)
    total = jnp.zeros((128, 128), F32)
    for dy in range(3):
        for dx in range(3):
            k = (3 * dy + dx) * 512
            total += jnp.dot(
                in_ref[dx, 32 * dy : 32 * dy + 128, :], teacher_ref[k : k + 512, :], preferred_element_type=F32
            )
    own = pl.ds(pl.multiple_of(col * 128, 128), 128)
    anchor = raw_ref[32:160, own]
    middle = anchor + delta(steps_ref, 0) * total
    second = silu(middle + wave_ref[1:2, own])
    line = lax.broadcasted_iota(jnp.int32, (128, 128), 0)
    inside = ((line >= 32) | (row > 0)) & ((line < 96) | (row < last))
    sec_ref[0:128, :] = jnp.where(inside, second, 0.0).astype(BF)
    mid_ref[...] = middle[32:96]
    anchor_ref[...] = anchor[32:96]
    lit_ref[...] = in_ref[:, 32:160, :]
    for copy in copies[3:]:
        copy.wait()


def second_kernel(
    sec_ref, teacher_ref, student_ref, mid_ref, anchor_ref, lit_ref, steps_ref, fine_ref, out_ref, in_ref, sems
):
    moves = [
        (fine_ref.at[:, 128 * n : 128 * n + 128], out_ref.at[128 + 256 * n : 384 + 256 * n, :]) for n in range(2)
    ]
    copies = start_all(moves, sems)
    field = jnp.concatenate([sec_ref[s, 0:128, :] for s in range(4)], axis=1).astype(F32).reshape(4, 32, 512)
    for at, step in enumerate((-1, 0, 1)):
        in_ref[at] = shifted(field, step).astype(BF).reshape(128, 512)
    total = jnp.zeros((64, 128), F32)
    for dy in range(3):
        for dx in range(3):
            k = (3 * dy + dx) * 512
            total += jnp.dot(
                in_ref[dx, 32 * dy : 32 * dy + 64, :], teacher_ref[k : k + 512, :], preferred_element_type=F32
            )
    pupil = jnp.zeros((64, 128), F32)
    for dy in range(3):
        for dx in range(3):
            k = (3 * dy + dx) * 512
            pupil += jnp.dot(
                lit_ref[dx, 32 * dy : 32 * dy + 64, :], student_ref[k : k + 512, :], preferred_element_type=F32
            )
    one, two = delta(steps_ref, 0), delta(steps_ref, 1)
    target = mid_ref[...] + two * total
    out_ref[0:64, :] = target.astype(BF)
    out_ref[64:128, :] = (target - (anchor_ref[...] + (one + two) * pupil)).astype(BF)
    for copy in copies:
        copy.wait()


def repeater():
    place = lax.broadcasted_iota(jnp.int32, (128, 32), 0) // 4
    return (place == lax.broadcasted_iota(jnp.int32, (128, 32), 1)).astype(BF)


def lifted(target, proj):
    wide = jnp.dot(repeater(), target, preferred_element_type=F32).astype(BF)
    return lax.dot_general(wide, proj, (((1,), (1,)), ((), ())), preferred_element_type=F32)


def grad_kernel(
    near_ref, sec_ref, late_ref, part_ref, field_ref, one_ref, two_ref, gap_ref, line_ref, sum_ref, gap_scratch
):
    row, col = lax.axis_index("rows"), lax.axis_index("cols")
    above, below, _ = near_at(row)
    even = row % 2 == 0
    pair = pl.multiple_of((col // 2) * 128, 128)
    lanes = pl.ds(pair, 128)
    target = jnp.concatenate([late_ref[s, 0:64, :] for s in range(4)], axis=1)
    proj = jnp.concatenate(
        [
            jnp.concatenate([sec_ref[s, 640 + 64 * n : 704 + 64 * n, :] for n in range(4)], axis=1)
            for s in range(4)
        ],
        axis=0,
    )
    for m in range(2):
        lift = lifted(target[32 * m : 32 * m + 32], proj)
        for i in range(4 * m, 4 * m + 4):
            noisy = jnp.concatenate(
                [
                    jnp.concatenate(
                        [late_ref[s, at + 32 * i : at + 32 * i + 32, :] for at in (128, 384)], axis=1
                    )
                    for s in range(4)
                ],
                axis=0,
            )
            line_ref[128 * i : 128 * i + 128, :] = (noisy.astype(F32) + lift).astype(BF)
    begin = pl.multiple_of(32 * col, 32)
    before = pl.multiple_of(jnp.maximum(32 * col - 16, 0), 16)
    after = pl.multiple_of(jnp.minimum(32 * col + 32, 112), 16)
    for i in range(8):
        for at, to, size in ((before, 0, 16), (begin, 16, 32), (after, 48, 16)):
            field_ref[i, to : to + size, :] = line_ref[pl.ds(128 * i + at, size), :]
    one_ref[...] = jnp.where(even, field_ref[7], field_ref[0])
    two_ref[...] = jnp.where(even, field_ref[0], field_ref[7])
    gap_scratch[...] = jnp.concatenate([late_ref[s, 64:128, :] for s in range(4)], axis=1).astype(F32)
    gap_ref[...] = jnp.concatenate(
        [gap_scratch[pl.ds(pl.multiple_of(32 * i + 8 * col, 8), 8), :] for i in range(2)], axis=0
    ).astype(BF)
    lines = [near_ref[s, pl.ds(above + 32, 32), lanes] for s in range(4)]
    for i in range(8):
        lines += [sec_ref[s, pl.ds(128 + 32 * i + 2 * pair, 32), :] for s in range(4)]
    lines += [near_ref[s, pl.ds(below + 32, 32), lanes] for s in range(4)]
    cot = jnp.concatenate(lines, axis=0).astype(F32)
    cot = jnp.where(col % 2 == 1, cot[:, 64:128], cot[:, 0:64]).reshape(10, 128, 64)
    moved = jnp.concatenate([shifted(cot, -dx) for dx in (-1, 0, 1)], axis=2).astype(BF).reshape(1280, 192)
    field = line_ref[...].T
    for dy in (-1, 0, 1):
        term = jnp.dot(field, moved[(1 - dy) * 128 : (1 - dy) * 128 + 1024], preferred_element_type=F32)
        for dx in range(3):
            one = term[:, 64 * dx : 64 * dx + 64]
            at = (3 * (dy + 1) + dx) * 256
            sum_ref[at : at + 256, :] = jnp.concatenate([one, one], axis=1)
    owners = part_ref.shape[0]
    each = 2304 // owners
    lane = lax.broadcasted_iota(jnp.int32, (owners, 128), 1)

    def line(j):
        if 2 * j >= each:
            return jnp.zeros((owners, 128), F32)
        even_line = sum_ref[pl.ds(2 * j, owners, stride=each), :]
        odd_line = sum_ref[pl.ds(2 * j + 1, owners, stride=each), :]
        return jnp.where(lane < 64, even_line, odd_line)

    for j in range(5):
        part_ref[:, :, 128 * j : 128 * j + 128] = jnp.stack([line(j), line(j + 5)], axis=1).astype(BF)
def share_kernel(scale, part_ref, share_ref):
    total = jnp.sum(part_ref[...].astype(F32), axis=0) * scale
    rows = []
    for j in range(9):
        line = total[j // 5 : j // 5 + 1, 128 * (j % 5) : 128 * (j % 5) + 128]
        rows += [line[:, 0:64], line[:, 64:128]]
    own = jnp.concatenate(rows + [jnp.zeros((14, 64), F32)], axis=0)
    high = own.astype(BF).astype(F32)
    share_ref[...] = jnp.concatenate([high, own - high], axis=1).astype(BF)


def fine_kernel(
    near_ref, sec_ref, turned_ref, beside_ref, across_ref, corner_ref, share_ref, field_ref, one_ref, two_ref,
    out_ref, back_ref, grad_ref,
    weight_ref, tile_ref, in_ref,
):
    row, col = lax.axis_index("rows"), lax.axis_index("cols")
    even = row % 2 == 0
    above, below, _ = near_at(row)
    owned = [share_ref[s, 0:32, :].astype(F32) for s in range(4)]
    grad_ref[...] = jnp.concatenate([(own[:, 0:64] + own[:, 64:128])[0:18] for own in owned], axis=1)
    for k, block in enumerate((turned_ref, beside_ref, across_ref, corner_ref)):
        tile = jnp.bitwise_xor(col, k)
        weight_ref[pl.ds(pl.multiple_of(64 * tile, 64), 64), :] = block[...]
    place = lax.broadcasted_iota(jnp.int32, (10, 64, 256), 1)
    framed = ((place >= 16) | (col > 0)) & ((place < 48) | (col < 3))

    def lay_out():
        wide = jnp.where(framed, tile_ref[...].astype(F32), 0.0)
        for at in range(3):
            in_ref[at] = wide[:, 15 + at : 47 + at].astype(BF).reshape(320, 256)

    one, two = one_ref[...], two_ref[...]
    tile_ref[0] = jnp.where(even, two, one)
    tile_ref[9] = jnp.where(even, one, two)
    tile_ref[1:9] = field_ref[...]
    lay_out()
    total = jnp.zeros((256, 256), F32)
    for dy in range(3):
        for dx in range(3):
            k = (3 * dy + dx) * 256
            total += lax.dot_general(
                in_ref[dx, 32 * dy : 32 * dy + 256, :],
                weight_ref[:, k : k + 256],
                (((1,), (1,)), ((), ())),
                preferred_element_type=F32,
            )
    out_ref[...] = total.astype(BF)

    left, right = jnp.maximum(col - 1, 0), jnp.minimum(col + 1, 3)
    for tile, at, to, size in ((left, 16, 0, 16), (col, 0, 16, 32), (right, 0, 48, 16)):
        for i, start in ((0, above), (9, below)):
            tile_ref[i, to : to + size, :] = near_ref[tile, pl.ds(start + 32 + at, size), :]
        for i in range(8):
            for half in range(2):
                first = 128 + 256 * half + 32 * i + at
                tile_ref[i + 1, to : to + size, 128 * half : 128 * half + 128] = sec_ref[tile, first : first + size, :]
    lay_out()
    total = jnp.zeros((256, 256), F32)
    for dy in range(3):
        for dx in range(3):
            k = (3 * dy + dx) * 256
            total += jnp.dot(
                in_ref[2 - dx, 32 * (2 - dy) : 32 * (2 - dy) + 256, :],
                weight_ref[:, k : k + 256],
                preferred_element_type=F32,
            )
    back_ref[...] = total.astype(BF)


def on_device(
    fine_noisy, fine_weight, projection, mid_noisy, teacher_weight, student_weight, steps, cotangent
):
    count = lax.axis_size("rows")
    near_pairs = [(i ^ 1, i) for i in range(count)]
    far_pairs = [(i, i + 1 if i % 2 else i - 1) for i in range(1, count - 1)]

    flat = cotangent.reshape(256, 256)
    one, two = call(
        pack_kernel,
        [shape((64, 256), BF), shape((64, 256), BF)],
        [pltpu.SemaphoreType.DMA((6,))],
        20000 * MIB,
        56,
        "pack",
        [pl.ANY] * 2,
    )(flat, mid_noisy.reshape(16, 512))
    two = lax.ppermute(two, "rows", far_pairs)
    pairs = [[i, i + 1] for i in range(0, count, 2)]
    one = lax.all_gather(one, "rows", axis=0, tiled=True, axis_index_groups=pairs)
    near = lax.all_gather(jnp.concatenate([one, two], axis=0), "cols", axis=0)
    steps = steps.reshape(1, 3)
    sec, middle, anchor, lit = call(
        first_kernel,
        [shape((896, 128), BF), shape((64, 128), F32), shape((64, 128), F32), shape((3, 128, 512), BF)],
        [
            pltpu.VMEM((3, 4, 32, 256), BF),
            pltpu.VMEM((192, 512), F32),
            pltpu.VMEM((2, 512), F32),
            pltpu.VMEM((3, 192, 512), BF),
            pltpu.SemaphoreType.DMA((9,)),
        ],
        300 * MIB,
        16,
        "first",
        [pl.ANY] + [pltpu.VMEM] * 2 + [pl.ANY] * 2,
    )(near, teacher_weight, steps, flat, projection.T)
    sec = lax.all_gather(sec, "cols", axis=0)
    (late,) = call(
        second_kernel,
        [shape((640, 128), BF)],
        [pltpu.VMEM((3, 128, 512), BF), pltpu.SemaphoreType.DMA((2,))],
        100 * MIB,
        16,
        "second",
        [pltpu.VMEM] * 7 + [pl.ANY],
    )(sec, teacher_weight, student_weight, middle, anchor, lit, steps, fine_noisy.reshape(256, 256))
    late = lax.all_gather(late, "cols", axis=0)
    part, field, one, two, gap = call(
        grad_kernel,
        [
            shape((count, 2, 640), BF),
            shape((8, 64, 256), BF),
            shape((64, 256), BF),
            shape((64, 256), BF),
            shape((16, 512), BF),
        ],
        [pltpu.VMEM((1024, 256), BF), pltpu.VMEM((2304, 128), F32), pltpu.VMEM((64, 512), F32)],
        1000 * MIB,
        32,
        "grad",
        [pltpu.VMEM] * 3,
    )(near, sec, late)
    turned, one, two, part = lax.optimization_barrier((fine_weight.T, one, two, part))
    part = lax.all_to_all(part, "rows", 0, 0, tiled=True)
    across = lax.ppermute(turned, "cols", [(i, i ^ 2) for i in range(4)])
    beside = lax.ppermute(turned, "cols", [(i, i ^ 1) for i in range(4)])
    two = lax.ppermute(two, "rows", far_pairs)
    one = lax.ppermute(one, "rows", near_pairs)
    corner = lax.ppermute(turned, "cols", [(i, i ^ 3) for i in range(4)])
    (share,) = call(
        functools.partial(share_kernel, 1.0 / math.sqrt(1024 * count)),
        [shape((32, 128), BF)],
        [],
        MIB,
        8,
        "share",
        [pltpu.VMEM],
    )(part)
    share = lax.all_gather(share, "cols", axis=0)
    share, one, two, across, beside, corner = lax.optimization_barrier((share, one, two, across, beside, corner))
    fine_out, grad_input, grad_weight = call(
        fine_kernel,
        [shape((256, 256), BF), shape((256, 256), BF), shape((18, 256), F32)],
        [pltpu.VMEM((256, 2304), BF), pltpu.VMEM((10, 64, 256), BF), pltpu.VMEM((3, 320, 256), BF)],
        1000 * MIB,
        32,
        "fine",
        [pltpu.VMEM] * 10,
    )(near, sec, turned, beside, across, corner, share, field, one, two)
    return (
        fine_out.reshape(8, 32, 256),
        grad_input.reshape(8, 32, 256),
        grad_weight,
        gap.reshape(2, 8, 512),
    )


def solution(mesh):
    placed = (
        P("rows", "cols", None),
        P(None, "cols"),
        P(None, "cols"),
        P("rows", "cols", None),
        P(None, "cols"),
        P(None, "cols"),
        P(),
        P("rows", "cols", None),
    )
    return jax.shard_map(
        on_device,
        mesh=mesh,
        in_specs=placed,
        out_specs=(
            P("rows", "cols", None),
            P("rows", "cols", None),
            P("rows", None),
            P("rows", "cols", None),
        ),
        check_vma=False,
    )
```
